512 devices in a mesh: seq: 64 (over z, x), head: 8 (over y, core).
Axes of the slice: x: 4, y: 4, z: 16, core: 2. Of those that a mesh axis runs over, the one named last changes fastest.
Arguments:
- query_rows: bfloat16 [16384, 4096], P('seq', 'head'), may hold values from -6 to 6
- key_rows: bfloat16 [16384, 4096], P('seq', 'head'), may hold values from -6 to 6
- value_rows: bfloat16 [16384, 4096], P('seq', 'head'), may hold values from -110 to 110
- feat_query: bfloat16 [32, 128, 128], P('head'), may hold values from -0.5 to 0.5
- feat_key: bfloat16 [32, 128, 128], P('head'), may hold values from -0.5 to 0.5
- norm_gain: float32 [4096], P('head'), may hold values from 0.25 to 1.75
- grad_out: bfloat16 [16384, 4096], P('seq', 'head'), may hold values from -6 to 6
Outputs:
- attended: bfloat16 [16384, 4096], P('seq', 'head')
- grad_query: bfloat16 [16384, 4096], P('seq', 'head')
- grad_key: bfloat16 [16384, 4096], P('seq', 'head')
- grad_value: bfloat16 [16384, 4096], P('seq', 'head')
- grad_feat_query: float32 [32, 128, 128], P('head')
- grad_feat_key: float32 [32, 128, 128], P('head')
- grad_gain: float32 [4096], P('head')
The draws below stay inside these ranges and needn't reach their ends.
All inputs are finite; a program needn't handle non-finite values.
Results may differ from the reference program's by a relative error of at most 0.017.
Values may be sent and summed in bfloat16 or wider, within the bound.
No kernel may reach another device: no remote copies, remote signals or barrier semaphores. Data moves between devices by JAX's collectives and lax.ppermute only.
A program may use at most 128 MiB of HBM per device.

```python
import math
import jax
import jax.numpy as jnp
from jax import lax

H = 32
DH = 128
TOK_DEV = 256
TOKENS = 16384
N_SEQ = 64


def draw_value_rows(key, part):
    first_key, second_key = jax.random.split(key, 2)
    columns = H * DH
    head_of = (jnp.arange(columns) // DH).astype(jnp.float32)
    ramp = head_of / max(H - 1, 1)
    column_scale = jnp.exp(jax.random.uniform(second_key, (columns,), jnp.float32, 0.0, math.log(3.3)))
    base = jnp.clip(jax.random.normal(first_key, (TOKENS, columns), jnp.float32), -4.0, 4.0)
    result = base * (jnp.exp(ramp * math.log(3.0)) * column_scale)[None, :]
    return result.astype(jnp.bfloat16)


def shard_levels(stream_key, extent, shards, low, top_value):
    gain = 1.0
    for axis_at, parts in shards:
        draws = jax.random.uniform(jax.random.fold_in(jax.random.fold_in(stream_key, 6), axis_at), (parts,), jnp.float32, low / len(shards), top_value / len(shards))
        gain = gain * jnp.repeat(jnp.exp(draws), extent[axis_at] // parts).reshape((-1,) + (1,) * (len(extent) - 1 - axis_at))
    return gain


def gaussian(key, extent, scale, most, cuts=(), held_as=jnp.bfloat16):
    values = jax.random.normal(key, extent, jnp.float32) * scale
    if len(cuts) > 0:
        values = shard_levels(key, extent, cuts, -0.22, 0.18) * values
    return jnp.clip(values, min=-most, max=most).astype(held_as)


def setup_inputs(seed: int = 0) -> dict:
    streams_of = jax.random.split(jax.random.key(seed), 8)
    return {
        "query_rows": gaussian(streams_of[0], (TOKENS, H * DH), 1.0, 6.0, ((0, 64), (1, 8))),
        "key_rows": gaussian(streams_of[1], (TOKENS, H * DH), 1.0, 6.0, ((0, 64), (1, 8))),
        "value_rows": draw_value_rows(jax.random.fold_in(streams_of[7], 71), 0),
        "feat_query": gaussian(streams_of[3], (H, DH, DH), DH ** -0.5, 0.5, ((0, 8),)),
        "feat_key": gaussian(streams_of[4], (H, DH, DH), DH ** -0.5, 0.5, ((0, 8),)),
        "norm_gain": jnp.clip(1.0 + 0.15 * jax.random.normal(streams_of[5], (H * DH,), jnp.float32), 0.25, 1.75),
        "grad_out": gaussian(streams_of[6], (TOKENS, H * DH), 1.0, 6.0, ((0, 64), (1, 8))),
    }


EPSILON = 1e-05

def silu_slope(pre_act):
    sigmoid_val = jax.nn.sigmoid(pre_act)
    return sigmoid_val * (1.0 + pre_act * (1.0 - sigmoid_val))

def rounded(array):
    return lax.optimization_barrier(array.astype(jnp.bfloat16))

def widen(array):
    return array.astype(jnp.float32)

def featurize(block, weights):
    pre_act = jnp.einsum('thd,hde->the', widen(block), widen(weights))
    return (pre_act, rounded(jax.nn.silu(pre_act)))

def reference(query_rows, key_rows, value_rows, feat_query, feat_key, norm_gain, grad_out):
    group_count = N_SEQ

    def as_groups(array):
        return array.reshape(group_count, TOK_DEV, H, DH)
    queries = as_groups(query_rows)
    keys_all = as_groups(key_rows)
    values = as_groups(value_rows)
    cotangent = as_groups(grad_out)
    gain_cols = norm_gain.reshape(H, DH)
    positions = jnp.arange(TOK_DEV)
    causal = (positions[:, None] >= positions[None, :])[None]
    full_width = H * DH

    def group_state(inputs):
        key_block, value_block = inputs
        key_unused, key_feat = featurize(key_block, feat_key)
        return jnp.einsum('thd,the->hde', widen(key_feat), widen(value_block))
    states = lax.map(group_state, (keys_all, values))
    prior_all = jnp.concatenate([jnp.zeros_like(states[:1]), jnp.cumsum(states[:-1], axis=0)], axis=0)

    def forward_group(inputs):
        query_block, key_block, value_block, carried_state, cotan_block = inputs
        query_pre, query_feat = featurize(query_block, feat_query)
        key_pre, key_feat = featurize(key_block, feat_key)
        scores = jnp.einsum('thd,shd->hts', widen(query_feat), widen(key_feat))
        scores = rounded(jnp.where(causal, scores, 0.0))
        intra = jnp.einsum('hts,she->the', widen(scores), widen(value_block))
        carried = jnp.einsum('thd,hde->the', widen(query_feat), widen(rounded(carried_state)))
        pre_norm = intra + carried
        rms_rows = jnp.sqrt(lax.optimization_barrier(jnp.sum(pre_norm * pre_norm, axis=(1, 2))) / full_width + EPSILON)
        normed = pre_norm / rms_rows[:, None, None]
        attended = (normed * gain_cols).astype(jnp.bfloat16)
        cotan_wide = widen(cotan_block)
        scaled = cotan_wide * gain_cols
        slope_rows = lax.optimization_barrier(jnp.sum(scaled * normed, axis=(1, 2))) / full_width
        delta_pre = rounded((scaled - normed * slope_rows[:, None, None]) / rms_rows[:, None, None])
        back_local = jnp.einsum('thd,the->hde', widen(query_feat), widen(delta_pre))
        gain_part = lax.optimization_barrier(jnp.sum(cotan_wide * normed, axis=0))
        return (attended, delta_pre, back_local, gain_part)
    attended_all, delta_all, back_states, gain_parts = lax.map(forward_group, (queries, keys_all, values, prior_all, cotangent))
    later_all = jnp.concatenate([jnp.flip(jnp.cumsum(jnp.flip(back_states[1:], 0), axis=0), 0), jnp.zeros_like(back_states[:1])], axis=0)

    def backward_group(inputs):
        query_block, key_block, value_block, carried_state, later_state, delta_pre = inputs
        query_pre, query_feat = featurize(query_block, feat_query)
        key_pre, key_feat = featurize(key_block, feat_key)
        scores = jnp.einsum('thd,shd->hts', widen(query_feat), widen(key_feat))
        scores = rounded(jnp.where(causal, scores, 0.0))
        delta_wide = widen(delta_pre)
        value_wide = widen(value_block)
        back_scores = rounded(jnp.where(causal, jnp.einsum('the,she->hts', delta_wide, value_wide), 0.0))
        prior_wide = widen(rounded(carried_state))
        later_wide = widen(rounded(later_state))
        query_grad = jnp.einsum('hts,shd->thd', widen(back_scores), widen(key_feat)) + jnp.einsum('the,hde->thd', delta_wide, prior_wide)
        query_pre_grad = rounded(query_grad * silu_slope(query_pre))
        grad_query = jnp.einsum('the,hde->thd', widen(query_pre_grad), widen(feat_query)).astype(jnp.bfloat16)
        query_weight_part = jnp.einsum('thd,the->hde', widen(query_block), widen(query_pre_grad))
        key_grad = jnp.einsum('hts,thd->shd', widen(back_scores), widen(query_feat)) + jnp.einsum('the,hde->thd', value_wide, later_wide)
        key_pre_grad = rounded(key_grad * silu_slope(key_pre))
        grad_key = jnp.einsum('the,hde->thd', widen(key_pre_grad), widen(feat_key)).astype(jnp.bfloat16)
        key_weight_part = jnp.einsum('thd,the->hde', widen(key_block), widen(key_pre_grad))
        grad_value = (jnp.einsum('hts,the->she', widen(scores), delta_wide) + jnp.einsum('thd,hde->the', widen(key_feat), later_wide)).astype(jnp.bfloat16)
        return (grad_query, grad_key, grad_value, query_weight_part, key_weight_part)
    grad_query, grad_key, grad_value, query_parts, key_parts = lax.map(backward_group, (queries, keys_all, values, prior_all, later_all, delta_all))
    flat_shape = (group_count * TOK_DEV, H * DH)
    return (attended_all.reshape(flat_shape), grad_query.reshape(flat_shape), grad_key.reshape(flat_shape), grad_value.reshape(flat_shape), lax.optimization_barrier(jnp.sum(query_parts, axis=0)), lax.optimization_barrier(jnp.sum(key_parts, axis=0)), lax.optimization_barrier(jnp.sum(gain_parts, axis=0)).reshape(H * DH))
```

```python
import jax
import jax.numpy as jnp
from jax import lax
from jax.sharding import Mesh, PartitionSpec as P

EPSILON = 1e-05
BF = jnp.bfloat16
F32 = jnp.float32
NEAR = 8


def swap(x, axis):
    return lax.all_to_all(x, axis, 0, 0)


def everyone(x, axis):
    return swap(jnp.broadcast_to(x[None], (lax.axis_size(axis),) + x.shape), axis)


def masked_sum(parts, backward):
    place = lax.axis_index("far")
    index = jnp.arange(parts.shape[0])
    keep = index > place if backward else index < place
    return jnp.sum(jnp.where(keep[:, None, None], parts.astype(F32), 0.0), axis=0)


def within(parts, backward):
    count = parts.shape[0]
    order = range(count - 1, -1, -1) if backward else range(count)
    total = jnp.zeros(parts.shape[1:], F32)
    sums = [None] * count
    for i in order:
        sums[i] = total
        total = total + parts[i].astype(F32)
    return jnp.stack(sums), total


def silu_slope(pre_act):
    sigmoid_val = jax.nn.sigmoid(pre_act)
    return sigmoid_val * (1.0 + pre_act * (1.0 - sigmoid_val))


def featurize(block, weights):
    pre_act = jnp.einsum("thd,hde->the", block, weights, preferred_element_type=F32)
    return (pre_act, jax.nn.silu(pre_act).astype(BF))


def shards(query_rows, key_rows, value_rows, feat_query, feat_key, norm_gain, grad_out):
    token_count = query_rows.shape[0]
    head_local = feat_query.shape[0]
    head_size = feat_query.shape[1]
    near = lax.axis_size("near")
    far = lax.axis_size("far")
    full_width = head_local * head_size * lax.axis_size("head")
    shape_heads = (token_count, head_local, head_size)
    chunk = head_local * head_size // near
    queries = query_rows.reshape(shape_heads)
    keys_local = key_rows.reshape(shape_heads)
    values = value_rows.reshape(shape_heads)
    cotangent = grad_out.reshape(shape_heads)
    gain_cols = norm_gain.reshape(head_local, head_size)
    positions = jnp.arange(token_count)
    causal = (positions[:, None] >= positions[None, :])[None]
    key_pre, key_feat = featurize(keys_local, feat_key)
    local_state = jnp.einsum("thd,the->hde", key_feat, values, preferred_element_type=F32)
    parts = swap(local_state.astype(BF).reshape(near, chunk, head_size), "near")
    sums, total = within(parts, False)
    offset = masked_sum(everyone(total.astype(BF), "far"), False)
    carried_round = swap((sums + offset).astype(BF), "near").reshape(
        head_local, head_size, head_size
    )
    query_pre, query_feat = featurize(queries, feat_query)
    scores = jnp.einsum("thd,shd->hts", query_feat, key_feat, preferred_element_type=F32)
    scores = jnp.where(causal, scores, 0.0).astype(BF)
    intra = jnp.einsum("hts,she->the", scores, values, preferred_element_type=F32)
    pre_norm = intra + jnp.einsum(
        "thd,hde->the", query_feat, carried_round, preferred_element_type=F32
    )
    cotan_wide = cotangent.astype(F32)
    scaled = cotan_wide * gain_cols
    rows = jnp.stack(
        [jnp.sum(pre_norm * pre_norm, axis=(1, 2)), jnp.sum(scaled * pre_norm, axis=(1, 2))]
    )
    rows = jnp.sum(everyone(rows, "head"), axis=0)
    rms_rows = jnp.sqrt(rows[0] / full_width + EPSILON)
    slope = rows[1] / rms_rows / full_width
    normed = pre_norm / rms_rows[:, None, None]
    attended = (normed * gain_cols).astype(BF).reshape(token_count, -1)
    delta_pre = ((scaled - normed * slope[:, None, None]) / rms_rows[:, None, None]).astype(BF)
    gain_local = jnp.sum(cotan_wide * normed, axis=0).reshape(-1)
    back_local = jnp.einsum("thd,the->hde", query_feat, delta_pre, preferred_element_type=F32)
    back_scores = jnp.where(
        causal,
        jnp.einsum("the,she->hts", delta_pre, values, preferred_element_type=F32),
        0.0,
    ).astype(BF)
    query_grad = jnp.einsum(
        "hts,shd->thd", back_scores, key_feat, preferred_element_type=F32
    ) + jnp.einsum("the,hde->thd", delta_pre, carried_round, preferred_element_type=F32)
    query_pre_grad = (query_grad * silu_slope(query_pre)).astype(BF)
    grad_query = (
        jnp.einsum("the,hde->thd", query_pre_grad, feat_query, preferred_element_type=F32)
        .astype(BF)
        .reshape(token_count, -1)
    )
    query_weight_part = jnp.einsum(
        "thd,the->hde", queries, query_pre_grad, preferred_element_type=F32
    )
    gain_rows = 16
    gain_pad = jnp.zeros((near, gain_rows * head_size), F32)
    gain_pad = gain_pad.at[:, : gain_local.shape[0] // near].set(gain_local.reshape(near, -1))
    payload = jnp.concatenate(
        [
            back_local.astype(BF).reshape(near, chunk, head_size),
            query_weight_part.astype(BF).reshape(near, chunk, head_size),
            gain_pad.astype(BF).reshape(near, gain_rows, head_size),
        ],
        axis=1,
    )
    parts = swap(payload, "near")
    sums, total = within(parts[:, :chunk], True)
    side = jnp.sum(parts[:, chunk:].astype(F32), axis=0).astype(BF)
    slim = chunk // far
    payload = jnp.concatenate(
        [
            jnp.broadcast_to(total.astype(BF)[None], (far, chunk, head_size)),
            side[:chunk].reshape(far, slim, head_size),
            jnp.broadcast_to(side[None, chunk : chunk + 8], (far, 8, head_size)),
        ],
        axis=1,
    )
    parts_far = swap(payload, "far")
    offset = masked_sum(parts_far[:, :chunk], True)
    side = jnp.sum(parts_far[:, chunk:].astype(F32), axis=0).astype(BF)
    later_round = swap((sums + offset).astype(BF), "near").reshape(
        head_local, head_size, head_size
    )
    key_grad = jnp.einsum(
        "hts,thd->shd", back_scores, query_feat, preferred_element_type=F32
    ) + jnp.einsum("the,hde->thd", values, later_round, preferred_element_type=F32)
    key_pre_grad = (key_grad * silu_slope(key_pre)).astype(BF)
    key_weight_part = jnp.einsum(
        "thd,the->hde", keys_local, key_pre_grad, preferred_element_type=F32
    )
    parts = swap(key_weight_part.astype(BF).reshape(near, chunk, head_size), "near")
    total = jnp.sum(parts.astype(F32), axis=0).astype(BF)
    parts = everyone(jnp.concatenate([total, side[:slim]], axis=0), "far")
    total = jnp.sum(parts[:, :chunk].astype(F32), axis=0).astype(BF)
    done = everyone(
        jnp.concatenate([total, parts[:, chunk:].reshape(chunk, head_size), side[slim:]], axis=0),
        "near",
    ).astype(F32)
    grad_feat_key = done[:, :chunk].reshape(feat_key.shape)
    grad_feat_query = done[:, chunk : 2 * chunk].reshape(feat_query.shape)
    grad_gain = done[:, 2 * chunk, : gain_local.shape[0] // near].reshape(-1)
    grad_key = (
        jnp.einsum("the,hde->thd", key_pre_grad, feat_key, preferred_element_type=F32)
        .astype(BF)
        .reshape(token_count, -1)
    )
    grad_value = (
        (
            jnp.einsum("hts,the->she", scores, delta_pre, preferred_element_type=F32)
            + jnp.einsum("thd,hde->the", key_feat, later_round, preferred_element_type=F32)
        )
        .astype(BF)
        .reshape(token_count, -1)
    )
    return (attended, grad_query, grad_key, grad_value, grad_feat_query, grad_feat_key, grad_gain)


def solution(mesh):
    seq, head = mesh.devices.shape
    split = Mesh(mesh.devices.reshape(seq // NEAR, NEAR, head), ("far", "near", "head"))
    wide = P(("far", "near"), "head")
    per_head = P("head", None, None)
    in_specs = (wide, wide, wide, per_head, per_head, P("head"), wide)
    out_specs = (wide, wide, wide, wide, per_head, per_head, P("head"))
    return jax.shard_map(shards, mesh=split, in_specs=in_specs, out_specs=out_specs, check_vma=False)
```

```python
import jax
import jax.numpy as jnp
from jax import lax
from jax.experimental import pallas as pl
from jax.experimental.pallas import tpu as pltpu
from jax.sharding import Mesh, PartitionSpec as P

EPSILON = 1e-05
BF = jnp.bfloat16
F32 = jnp.float32
NEAR = 8
GAIN_ROWS = 16
STAT_ROWS = 8
VMEM_BYTES = 24 * 1024 * 1024


def swap(x, axis):
    return lax.all_to_all(x, axis, 0, 0)


def run(kernel, outs, ins, after=(), flops=10**8):
    count = len(ins)

    def body(*refs):
        kernel(*refs[:count], *refs[count + len(after) :])

    whole = pl.BlockSpec(memory_space=pltpu.VMEM)
    return pl.pallas_call(
        body,
        out_shape=[jax.ShapeDtypeStruct(shape, dtype) for shape, dtype in outs],
        in_specs=[whole] * count + [pl.BlockSpec(memory_space=pl.ANY)] * len(after),
        out_specs=[whole] * len(outs),
        compiler_params=pltpu.CompilerParams(vmem_limit_bytes=VMEM_BYTES),
        cost_estimate=pl.CostEstimate(flops=flops, bytes_accessed=10**6, transcendentals=0),
    )(*ins, *after)


def dot(a, b, over_a, over_b):
    return lax.dot_general(a, b, (((over_a,), (over_b,)), ((), ())), preferred_element_type=F32)


def silu_and_slope(x):
    g = 1.0 / (1.0 + jnp.exp(-x))
    return x * g, g * (1.0 + x * (1.0 - g))


def causal_mask(count):
    rows = lax.broadcasted_iota(jnp.int32, (count, count), 0)
    cols = lax.broadcasted_iota(jnp.int32, (count, count), 1)
    return rows >= cols


def shards(query_rows, key_rows, value_rows, feat_query, feat_key, norm_gain, grad_out):
    tokens, width = query_rows.shape
    heads, size = feat_query.shape[0], feat_query.shape[1]
    near, far = lax.axis_size("near"), lax.axis_size("far")
    full_width = width * lax.axis_size("head")
    chunk = heads * size // near
    slim = chunk // far
    per_head = near // heads
    gain_row = norm_gain.reshape(1, width)
    group = lax.axis_index("far").reshape(1)
    cols = [slice(h * size, (h + 1) * size) for h in range(heads)]

    def put_state(out_ref, h, value, row):
        for part in range(per_head):
            rows = value[part * chunk : (part + 1) * chunk]
            out_ref[h * per_head + part, row : row + chunk, :] = rows.astype(BF)

    def get_state(ref, h):
        parts = [ref[h * per_head + part] for part in range(per_head)]
        return jnp.concatenate(parts, axis=0)

    def state_kernel(k_ref, v_ref, w_ref, kf_ref, out_ref):
        for h, at in enumerate(cols):
            pre = dot(k_ref[:, at], w_ref[h], 1, 0)
            feat = (pre / (1.0 + jnp.exp(-pre))).astype(BF)
            kf_ref[:, at] = feat
            put_state(out_ref, h, dot(feat, v_ref[:, at], 0, 0), 0)

    key_feat, payload = run(
        state_kernel,
        [((tokens, width), BF), ((near, chunk, size), BF)],
        [key_rows, value_rows, feat_key],
    )
    parts = swap(payload, "near")

    def query_kernel(q_ref, wq_ref, k_ref, wk_ref, kf_ref, v_ref, qf_ref, qs_ref, ks_ref, sc_ref, intra_ref):
        mask = causal_mask(tokens)
        for h, at in enumerate(cols):
            act, slope = silu_and_slope(dot(q_ref[:, at], wq_ref[h], 1, 0))
            qs_ref[:, at] = slope
            feat = act.astype(BF)
            qf_ref[:, at] = feat
            ks_ref[:, at] = silu_and_slope(dot(k_ref[:, at], wk_ref[h], 1, 0))[1]
            scores = jnp.where(mask, dot(feat, kf_ref[:, at], 1, 1), 0.0).astype(BF)
            sc_ref[h] = scores
            intra_ref[:, at] = dot(scores, v_ref[:, at], 1, 0)

    query_feat, query_slope, key_slope, scores, intra = run(
        query_kernel,
        [
            ((tokens, width), BF),
            ((tokens, width), F32),
            ((tokens, width), F32),
            ((heads, tokens, tokens), BF),
            ((tokens, width), F32),
        ],
        [query_rows, feat_query, key_rows, feat_key, key_feat, value_rows],
        after=[group],
    )

    def total_kernel(in_ref, out_ref):
        total = in_ref[0].astype(F32)
        for i in range(1, near):
            total = total + in_ref[i].astype(F32)
        total = total.astype(BF)
        for i in range(out_ref.shape[0]):
            out_ref[i] = total

    (payload,) = run(total_kernel, [((far, chunk, size), BF)], [parts], after=[query_feat])
    parts_far = swap(payload, "far")

    def join(parts_ref, far_ref, group_ref, out_ref, backward):
        place = group_ref[0]
        state = jnp.zeros((chunk, size), F32)
        for i in range(far):
            keep = (i > place) if backward else (i < place)
            state = state + jnp.where(keep, far_ref[i][:chunk].astype(F32), 0.0)
        for i in range(near - 1, -1, -1) if backward else range(near):
            out_ref[i] = state.astype(BF)
            state = state + parts_ref[i][:chunk].astype(F32)

    def run_join(kernel, outs, ins):
        whole = pl.BlockSpec(memory_space=pltpu.VMEM)
        return pl.pallas_call(
            kernel,
            out_shape=[jax.ShapeDtypeStruct(shape, dtype) for shape, dtype in outs],
            in_specs=[whole] * (len(ins) - 1) + [pl.BlockSpec(memory_space=pltpu.SMEM)],
            out_specs=[whole] * len(outs),
            compiler_params=pltpu.CompilerParams(vmem_limit_bytes=VMEM_BYTES),
            cost_estimate=pl.CostEstimate(flops=10**6, bytes_accessed=10**6, transcendentals=0),
        )(*ins)

    def prior_kernel(parts_ref, far_ref, group_ref, out_ref):
        join(parts_ref, far_ref, group_ref, out_ref, False)

    (payload,) = run_join(prior_kernel, [((near, chunk, size), BF)], [parts, parts_far, group])
    prior = swap(payload, "near")

    def norm_kernel(qf_ref, p_ref, intra_ref, go_ref, gain_ref, pre_ref, out_ref):
        squares = jnp.zeros((tokens, size), F32)
        inner = jnp.zeros((tokens, size), F32)
        for h, at in enumerate(cols):
            pre = intra_ref[:, at] + dot(qf_ref[:, at], get_state(p_ref, h), 1, 0)
            pre_ref[:, at] = pre
            squares = squares + pre * pre
            inner = inner + go_ref[:, at].astype(F32) * gain_ref[:, at] * pre
        squares = jnp.sum(squares, axis=1, keepdims=True)
        inner = jnp.sum(inner, axis=1, keepdims=True)
        lane = lax.broadcasted_iota(jnp.int32, (tokens, size), 1)
        both = jnp.where(lane == 0, squares, jnp.where(lane == 1, inner, 0.0))
        rows = jnp.transpose(both)[:STAT_ROWS]
        for i in range(out_ref.shape[0]):
            out_ref[i] = rows

    peers = lax.axis_size("head")
    pre_norm, payload = run(
        norm_kernel,
        [((tokens, width), F32), ((peers, STAT_ROWS, tokens), F32)],
        [query_feat, prior, intra, grad_out, gain_row],
    )
    stats = swap(payload, "head")

    def row_factors(st_ref):
        rows = st_ref[0]
        for i in range(1, peers):
            rows = rows + st_ref[i]
        rows = jnp.concatenate([rows, jnp.zeros((size - STAT_ROWS, tokens), F32)], axis=0)
        both = jnp.transpose(rows)
        inverse = 1.0 / jnp.sqrt(both[:, 0:1] / full_width + EPSILON)
        return inverse, both[:, 1:2] * inverse / full_width

    def delta_kernel(
        st_ref, pre_ref, go_ref, gain_ref, qf_ref, v_ref, kf_ref, p_ref, qs_ref, q_ref,
        delta_ref, bs_ref, qg_ref, out_ref,
    ):
        inverse, slope = row_factors(st_ref)
        mask = causal_mask(tokens)
        gains = []
        for h, at in enumerate(cols):
            wide = go_ref[:, at].astype(F32)
            normed = pre_ref[:, at] * inverse
            delta = ((wide * gain_ref[:, at] - normed * slope) * inverse).astype(BF)
            delta_ref[:, at] = delta
            gains.append(jnp.sum(wide * normed, axis=0, keepdims=True))
            put_state(out_ref, h, dot(qf_ref[:, at], delta, 0, 0), 0)
            back = jnp.where(mask, dot(delta, v_ref[:, at], 1, 1), 0.0).astype(BF)
            bs_ref[h] = back
            grad = dot(back, kf_ref[:, at], 1, 0) + dot(delta, get_state(p_ref, h), 1, 1)
            grad = (grad * qs_ref[:, at]).astype(BF)
            qg_ref[:, at] = grad
            put_state(out_ref, h, dot(q_ref[:, at], grad, 0, 0), chunk)
        rest = [jnp.zeros((GAIN_ROWS - heads, size), F32)]
        rows = jnp.concatenate(gains + rest, axis=0).astype(BF)
        for i in range(near):
            out_ref[i, 2 * chunk :, :] = rows

    delta, back_scores, query_pre_grad, payload = run(
        delta_kernel,
        [
            ((tokens, width), BF),
            ((heads, tokens, tokens), BF),
            ((tokens, width), BF),
            ((near, 2 * chunk + GAIN_ROWS, size), BF),
        ],
        [stats, pre_norm, grad_out, gain_row, query_feat, value_rows, key_feat, prior, query_slope, query_rows],
    )
    parts = swap(payload, "near")

    def local_kernel(
        st_ref, pre_ref, gain_ref, qg_ref, wq_ref, bs_ref, qf_ref, sc_ref, delta_ref,
        att_ref, gq_ref, kg_ref, gv_ref,
    ):
        inverse, _ = row_factors(st_ref)
        for h, at in enumerate(cols):
            att_ref[:, at] = (pre_ref[:, at] * inverse * gain_ref[:, at]).astype(BF)
            gq_ref[:, at] = dot(qg_ref[:, at], wq_ref[h], 1, 1).astype(BF)
            kg_ref[:, at] = dot(bs_ref[h], qf_ref[:, at], 0, 0)
            gv_ref[:, at] = dot(sc_ref[h], delta_ref[:, at], 0, 0)

    attended, grad_query, key_grad_local, grad_value_local = run(
        local_kernel,
        [((tokens, width), BF), ((tokens, width), BF), ((tokens, width), F32), ((tokens, width), F32)],
        [stats, pre_norm, gain_row, query_pre_grad, feat_query, back_scores, query_feat, scores, delta],
    )

    def back_total_kernel(in_ref, out_ref):
        total = in_ref[0].astype(F32)
        for i in range(1, near):
            total = total + in_ref[i].astype(F32)
        head_rows, gains = total[:chunk], total[2 * chunk : 2 * chunk + 8]
        for i in range(far):
            part = total[chunk + i * slim : chunk + (i + 1) * slim]
            out_ref[i] = jnp.concatenate([head_rows, part, gains], axis=0).astype(BF)

    (payload,) = run(
        back_total_kernel, [((far, chunk + slim + 8, size), BF)], [parts], after=[grad_query]
    )
    parts_far = swap(payload, "far")

    def later_kernel(parts_ref, far_ref, group_ref, out_ref, side_ref):
        join(parts_ref, far_ref, group_ref, out_ref, True)
        side = far_ref[0].astype(F32)[chunk:]
        for i in range(1, far):
            side = side + far_ref[i].astype(F32)[chunk:]
        side_ref[...] = side

    payload, side = run_join(
        later_kernel,
        [((near, chunk, size), BF), ((slim + 8, size), F32)],
        [parts, parts_far, group],
    )
    grad_gain = side[slim : slim + heads].reshape(width)
    later = swap(payload, "near")

    def key_kernel(kg_ref, v_ref, l_ref, ks_ref, k_ref, kpg_ref, out_ref):
        for h, at in enumerate(cols):
            grad = kg_ref[:, at] + dot(v_ref[:, at], get_state(l_ref, h), 1, 1)
            grad = (grad * ks_ref[:, at]).astype(BF)
            kpg_ref[:, at] = grad
            put_state(out_ref, h, dot(k_ref[:, at], grad, 0, 0), 0)

    key_pre_grad, payload = run(
        key_kernel,
        [((tokens, width), BF), ((near, chunk, size), BF)],
        [key_grad_local, value_rows, later, key_slope, key_rows],
    )
    parts = swap(payload, "near")

    def last_kernel(kpg_ref, wk_ref, gv_ref, kf_ref, l_ref, gk_ref, out_ref):
        for h, at in enumerate(cols):
            gk_ref[:, at] = dot(kpg_ref[:, at], wk_ref[h], 1, 1).astype(BF)
            value = gv_ref[:, at] + dot(kf_ref[:, at], get_state(l_ref, h), 1, 0)
            out_ref[:, at] = value.astype(BF)

    grad_key, grad_value = run(
        last_kernel,
        [((tokens, width), BF), ((tokens, width), BF)],
        [key_pre_grad, feat_key, grad_value_local, key_feat, later],
    )

    def weight_total_kernel(in_ref, side_ref, out_ref):
        total = in_ref[0].astype(F32)
        for i in range(1, near):
            total = total + in_ref[i].astype(F32)
        pad = jnp.zeros((8, size), F32)
        total = jnp.concatenate([total, side_ref[:slim], pad], axis=0).astype(BF)
        for i in range(far):
            out_ref[i] = total

    (payload,) = run(
        weight_total_kernel,
        [((far, chunk + slim + 8, size), BF)],
        [parts, side],
        after=[grad_key],
    )
    parts_far = swap(payload, "far")

    def weight_kernel(far_ref, out_ref):
        total = far_ref[0].astype(F32)[:chunk]
        for i in range(1, far):
            total = total + far_ref[i].astype(F32)[:chunk]
        queries = [far_ref[i].astype(F32)[chunk : chunk + slim] for i in range(far)]
        total = jnp.concatenate([total] + queries, axis=0).astype(BF)
        for i in range(near):
            out_ref[i] = total

    (payload,) = run(weight_kernel, [((near, 2 * chunk, size), BF)], [parts_far])
    done = swap(payload, "near")

    def widen_kernel(in_ref, gq_ref, gk_ref):
        for h in range(heads):
            for part in range(per_head):
                rows = slice(part * chunk, (part + 1) * chunk)
                gk_ref[h, rows] = in_ref[h * per_head + part, :chunk].astype(F32)
                gq_ref[h, rows] = in_ref[h * per_head + part, chunk:].astype(F32)

    grad_feat_query, grad_feat_key = run(
        widen_kernel, [(feat_query.shape, F32), (feat_key.shape, F32)], [done]
    )
    return (attended, grad_query, grad_key, grad_value, grad_feat_query, grad_feat_key, grad_gain)


def solution(mesh):
    seq, head = mesh.devices.shape
    split = Mesh(mesh.devices.reshape(seq // NEAR, NEAR, head), ("far", "near", "head"))
    wide = P(("far", "near"), "head")
    per_head = P("head", None, None)
    in_specs = (wide, wide, wide, per_head, per_head, P("head"), wide)
    out_specs = (wide, wide, wide, wide, per_head, per_head, P("head"))
    return jax.shard_map(shards, mesh=split, in_specs=in_specs, out_specs=out_specs, check_vma=False)
```

```python
import jax
import jax.numpy as jnp
from jax import lax
from jax.experimental import pallas as pl
from jax.experimental.pallas import tpu as pltpu
from jax.sharding import Mesh, PartitionSpec as P

EPSILON = 1e-05
BF = jnp.bfloat16
F32 = jnp.float32
NEAR = 8
GAIN_ROWS = 16
STAT_ROWS = 8
TOKEN = ((8, 128), F32)
VMEM_BYTES = 24 * 1024 * 1024
WHOLE_VMEM = 64 * 1024 * 1024


def swap(x, axis):
    return lax.all_to_all(x, axis, 0, 0)


def run(kernel, outs, ins, after=(), fetch=(), limit=VMEM_BYTES):
    count, copies = len(ins), len(fetch)

    def body(*refs):
        sources = refs[count : count + copies]
        outputs = refs[count + copies + len(after) : count + copies + len(after) + len(outs)]
        if not copies:
            return kernel(*refs[:count], *outputs)
        held, sems = refs[-copies - 1 : -1], refs[-1]
        moves = [pltpu.make_async_copy(sources[i], held[i], sems.at[i]) for i in range(copies)]
        for move in moves:
            move.start()
        return kernel(*refs[:count], *held, *outputs, [move.wait for move in moves])

    whole = pl.BlockSpec(memory_space=pltpu.VMEM)
    far_off = pl.BlockSpec(memory_space=pl.ANY)
    scratch = [pltpu.VMEM(x.shape, x.dtype) for x in fetch]
    return pl.pallas_call(
        body,
        out_shape=[jax.ShapeDtypeStruct(shape, dtype) for shape, dtype in outs],
        in_specs=[whole] * count
        + [far_off] * copies
        + [far_off] * len(after),
        out_specs=[whole] * len(outs),
        scratch_shapes=scratch + [pltpu.SemaphoreType.DMA((copies,))] if copies else [],
        compiler_params=pltpu.CompilerParams(vmem_limit_bytes=limit),
        cost_estimate=pl.CostEstimate(flops=10**8, bytes_accessed=10**6, transcendentals=0),
    )(*ins, *fetch, *after)


def dot(a, b, over_a, over_b):
    return lax.dot_general(a, b, (((over_a,), (over_b,)), ((), ())), preferred_element_type=F32)


def silu_slope(x):
    g = 1.0 / (1.0 + jnp.exp(-x))
    return g * (1.0 + x * (1.0 - g))


def causal_mask(count):
    rows = lax.broadcasted_iota(jnp.int32, (count, count), 0)
    cols = lax.broadcasted_iota(jnp.int32, (count, count), 1)
    return rows >= cols


def shards(query_rows, key_rows, value_rows, feat_query, feat_key, norm_gain, grad_out):
    tokens, width = query_rows.shape
    heads, size = feat_query.shape[0], feat_query.shape[1]
    near, far = lax.axis_size("near"), lax.axis_size("far")
    full_width = width * lax.axis_size("head")
    chunk = heads * size // near
    slim = chunk // far
    per_head = near // heads
    gain_row = norm_gain.reshape(1, width)
    group = lax.axis_index("far").reshape(1)
    cols = [slice(h * size, (h + 1) * size) for h in range(heads)]

    def put_state(out_ref, h, value, row):
        for part in range(per_head):
            rows = value[part * chunk : (part + 1) * chunk]
            out_ref[h * per_head + part, row : row + chunk, :] = rows.astype(BF)

    def get_state(ref, h):
        parts = [ref[h * per_head + part] for part in range(per_head)]
        return jnp.concatenate(parts, axis=0)

    def state_kernel(w_ref, k_ref, v_ref, kf_ref, out_ref, waits):
        waits[0]()
        waits[1]()
        for h, at in enumerate(cols):
            pre = dot(k_ref[:, at], w_ref[h], 1, 0)
            kf_ref[:, at] = (pre / (1.0 + jnp.exp(-pre))).astype(BF)
        waits[2]()
        for h, at in enumerate(cols):
            put_state(out_ref, h, dot(kf_ref[:, at], v_ref[:, at], 0, 0), 0)

    key_feat, payload = run(
        state_kernel,
        [((tokens, width), BF), ((near, chunk, size), BF)],
        [],
        fetch=[feat_key, key_rows, value_rows],
        limit=WHOLE_VMEM,
    )
    parts = swap(payload, "near")

    def query_kernel(kf_ref, wq_ref, q_ref, v_ref, gain_ref, qf_ref, intra_ref, gain_out):
        gain_out[...] = gain_ref[...]
        mask = causal_mask(tokens)
        for h, at in enumerate(cols):
            pre = dot(q_ref[:, at], wq_ref[h], 1, 0)
            feat = (pre / (1.0 + jnp.exp(-pre))).astype(BF)
            qf_ref[:, at] = feat
            scores = jnp.where(mask, dot(feat, kf_ref[:, at], 1, 1), 0.0).astype(BF)
            intra_ref[:, at] = dot(scores, v_ref[:, at], 1, 0)

    query_feat, intra, gain_row = run(
        query_kernel,
        [((tokens, width), BF), ((tokens, width), F32), ((1, width), F32)],
        [key_feat, feat_query, query_rows, value_rows, gain_row],
        after=[group],
    )

    def total_kernel(in_ref, out_ref):
        total = in_ref[0].astype(F32)
        for i in range(1, near):
            total = total + in_ref[i].astype(F32)
        total = total.astype(BF)
        for i in range(out_ref.shape[0]):
            out_ref[i] = total

    (payload,) = run(total_kernel, [((far, chunk, size), BF)], [parts], after=[query_feat])
    parts_far = swap(payload, "far")

    def join(parts_ref, far_ref, group_ref, out_ref, backward):
        place = group_ref[0]
        state = jnp.zeros((chunk, size), F32)
        for i in range(far):
            keep = (i > place) if backward else (i < place)
            state = state + jnp.where(keep, far_ref[i][:chunk].astype(F32), 0.0)
        for i in range(near - 1, -1, -1) if backward else range(near):
            out_ref[i] = state.astype(BF)
            state = state + parts_ref[i][:chunk].astype(F32)

    def run_join(kernel, outs, ins):
        whole = pl.BlockSpec(memory_space=pltpu.VMEM)
        return pl.pallas_call(
            kernel,
            out_shape=[jax.ShapeDtypeStruct(shape, dtype) for shape, dtype in outs],
            in_specs=[whole] * (len(ins) - 1) + [pl.BlockSpec(memory_space=pltpu.SMEM)],
            out_specs=[whole] * len(outs),
            compiler_params=pltpu.CompilerParams(vmem_limit_bytes=VMEM_BYTES),
            cost_estimate=pl.CostEstimate(flops=10**6, bytes_accessed=10**6, transcendentals=0),
        )(*ins)

    def prior_kernel(parts_ref, far_ref, group_ref, out_ref):
        join(parts_ref, far_ref, group_ref, out_ref, False)

    (payload,) = run_join(prior_kernel, [((near, chunk, size), BF)], [parts, parts_far, group])
    prior = swap(payload, "near")

    def norm_kernel(qf_ref, p_ref, intra_ref, go_ref, gain_ref, pre_ref, out_ref):
        squares = jnp.zeros((tokens, size), F32)
        inner = jnp.zeros((tokens, size), F32)
        for h, at in enumerate(cols):
            pre = intra_ref[:, at] + dot(qf_ref[:, at], get_state(p_ref, h), 1, 0)
            pre_ref[:, at] = pre
            squares = squares + pre * pre
            inner = inner + go_ref[:, at].astype(F32) * gain_ref[:, at] * pre
        squares = jnp.sum(squares, axis=1, keepdims=True)
        inner = jnp.sum(inner, axis=1, keepdims=True)
        lane = lax.broadcasted_iota(jnp.int32, (tokens, size), 1)
        both = jnp.where(lane == 0, squares, jnp.where(lane == 1, inner, 0.0))
        rows = jnp.transpose(both)[:STAT_ROWS]
        for i in range(out_ref.shape[0]):
            out_ref[i] = rows

    peers = lax.axis_size("head")
    pre_norm, payload = run(
        norm_kernel,
        [((tokens, width), F32), ((peers, STAT_ROWS, tokens), F32)],
        [query_feat, prior, intra, grad_out, gain_row],
    )
    stats = swap(payload, "head")

    def row_factors(st_ref):
        rows = st_ref[0]
        for i in range(1, peers):
            rows = rows + st_ref[i]
        rows = jnp.concatenate([rows, jnp.zeros((size - STAT_ROWS, tokens), F32)], axis=0)
        both = jnp.transpose(rows)
        inverse = 1.0 / jnp.sqrt(both[:, 0:1] / full_width + EPSILON)
        return inverse, both[:, 1:2] * inverse / full_width

    def delta_of(at, inverse, slope, pre_ref, go_ref, gain_ref):
        normed = pre_ref[:, at] * inverse
        wide = go_ref[:, at].astype(F32)
        return ((wide * gain_ref[:, at] - normed * slope) * inverse).astype(BF), wide, normed

    def query_side(h, at, delta, mask, v_ref, kf_ref, p_ref, q_ref, wq_ref):
        back = jnp.where(mask, dot(delta, v_ref[:, at], 1, 1), 0.0).astype(BF)
        grad = dot(back, kf_ref[:, at], 1, 0) + dot(delta, get_state(p_ref, h), 1, 1)
        return back, (grad * silu_slope(dot(q_ref[:, at], wq_ref[h], 1, 0))).astype(BF)

    def delta_kernel(st_ref, pre_ref, go_ref, gain_ref, qf_ref, v_ref, kf_ref, p_ref, q_ref, wq_ref, out_ref):
        inverse, slope = row_factors(st_ref)
        mask = causal_mask(tokens)
        gains = []
        for h, at in enumerate(cols):
            delta, wide, normed = delta_of(at, inverse, slope, pre_ref, go_ref, gain_ref)
            gains.append(jnp.sum(wide * normed, axis=0, keepdims=True))
            put_state(out_ref, h, dot(qf_ref[:, at], delta, 0, 0), 0)
            _, grad = query_side(h, at, delta, mask, v_ref, kf_ref, p_ref, q_ref, wq_ref)
            put_state(out_ref, h, dot(q_ref[:, at], grad, 0, 0), chunk)
        rest = [jnp.zeros((GAIN_ROWS - heads, size), F32)]
        rows = jnp.concatenate(gains + rest, axis=0).astype(BF)
        for i in range(near):
            out_ref[i, 2 * chunk :, :] = rows

    (payload,) = run(
        delta_kernel,
        [((near, 2 * chunk + GAIN_ROWS, size), BF)],
        [stats, pre_norm, grad_out, gain_row, query_feat, value_rows, key_feat, prior, query_rows, feat_query],
    )
    parts = swap(payload, "near")

    def local_kernel(
        st_ref, pre_ref, go_ref, gain_ref, qf_ref, v_ref, kf_ref, p_ref, q_ref, wq_ref,
        att_ref, gq_ref, kg_ref, gv_ref, token_ref,
    ):
        token_ref[...] = jnp.zeros(token_ref.shape, F32)
        inverse, slope = row_factors(st_ref)
        mask = causal_mask(tokens)
        for h, at in enumerate(cols):
            delta, _, normed = delta_of(at, inverse, slope, pre_ref, go_ref, gain_ref)
            att_ref[:, at] = (normed * gain_ref[:, at]).astype(BF)
            back, grad = query_side(h, at, delta, mask, v_ref, kf_ref, p_ref, q_ref, wq_ref)
            gq_ref[:, at] = dot(grad, wq_ref[h], 1, 1).astype(BF)
            kg_ref[:, at] = dot(back, qf_ref[:, at], 0, 0)
            scores = jnp.where(mask, dot(qf_ref[:, at], kf_ref[:, at], 1, 1), 0.0).astype(BF)
            gv_ref[:, at] = dot(scores, delta, 0, 0)

    attended, grad_query, key_grad_local, grad_value_local, token = run(
        local_kernel,
        [((tokens, width), BF)] * 2 + [((tokens, width), F32)] * 2 + [TOKEN],
        [stats, pre_norm, grad_out, gain_row, query_feat, value_rows, key_feat, prior, query_rows, feat_query],
    )

    def back_total_kernel(in_ref, out_ref):
        total = in_ref[0].astype(F32)
        for i in range(1, near):
            total = total + in_ref[i].astype(F32)
        head_rows, gains = total[:chunk], total[2 * chunk : 2 * chunk + 8]
        for i in range(far):
            part = total[chunk + i * slim : chunk + (i + 1) * slim]
            out_ref[i] = jnp.concatenate([head_rows, part, gains], axis=0).astype(BF)

    (payload,) = run(
        back_total_kernel, [((far, chunk + slim + 8, size), BF)], [parts], after=[token]
    )
    parts_far = swap(payload, "far")

    def later_kernel(parts_ref, far_ref, group_ref, out_ref, side_ref, gain_ref):
        join(parts_ref, far_ref, group_ref, out_ref, True)
        side = far_ref[0].astype(F32)[chunk:]
        for i in range(1, far):
            side = side + far_ref[i].astype(F32)[chunk:]
        side_ref[...] = side
        for h, at in enumerate(cols):
            gain_ref[:, at] = side[slim + h : slim + h + 1]

    payload, side, gain_sum = run_join(
        later_kernel,
        [((near, chunk, size), BF), ((slim + 8, size), F32), ((1, width), F32)],
        [parts, parts_far, group],
    )
    grad_gain = gain_sum.reshape(width)
    later = swap(payload, "near")

    def key_kernel(kg_ref, v_ref, l_ref, wk_ref, k_ref, kpg_ref, out_ref):
        for h, at in enumerate(cols):
            grad = kg_ref[:, at] + dot(v_ref[:, at], get_state(l_ref, h), 1, 1)
            grad = (grad * silu_slope(dot(k_ref[:, at], wk_ref[h], 1, 0))).astype(BF)
            kpg_ref[:, at] = grad
            put_state(out_ref, h, dot(k_ref[:, at], grad, 0, 0), 0)

    key_pre_grad, payload = run(
        key_kernel,
        [((tokens, width), BF), ((near, chunk, size), BF)],
        [key_grad_local, value_rows, later, feat_key, key_rows],
    )
    parts = swap(payload, "near")

    def last_kernel(kpg_ref, wk_ref, gv_ref, kf_ref, l_ref, gk_ref, out_ref, token_ref):
        token_ref[...] = jnp.zeros(token_ref.shape, F32)
        for h, at in enumerate(cols):
            gk_ref[:, at] = dot(kpg_ref[:, at], wk_ref[h], 1, 1).astype(BF)
            value = gv_ref[:, at] + dot(kf_ref[:, at], get_state(l_ref, h), 1, 0)
            out_ref[:, at] = value.astype(BF)

    grad_key, grad_value, token = run(
        last_kernel,
        [((tokens, width), BF), ((tokens, width), BF), TOKEN],
        [key_pre_grad, feat_key, grad_value_local, key_feat, later],
    )

    def weight_total_kernel(in_ref, side_ref, out_ref):
        total = in_ref[0].astype(F32)
        for i in range(1, near):
            total = total + in_ref[i].astype(F32)
        pad = jnp.zeros((8, size), F32)
        total = jnp.concatenate([total, side_ref[:slim], pad], axis=0).astype(BF)
        for i in range(far):
            out_ref[i] = total

    (payload,) = run(
        weight_total_kernel,
        [((far, chunk + slim + 8, size), BF)],
        [parts, side],
        after=[token, grad_gain],
    )
    parts_far = swap(payload, "far")

    def weight_kernel(far_ref, out_ref):
        total = far_ref[0].astype(F32)[:chunk]
        for i in range(1, far):
            total = total + far_ref[i].astype(F32)[:chunk]
        queries = [far_ref[i].astype(F32)[chunk : chunk + slim] for i in range(far)]
        total = jnp.concatenate([total] + queries, axis=0).astype(BF)
        for i in range(near):
            out_ref[i] = total

    (payload,) = run(weight_kernel, [((near, 2 * chunk, size), BF)], [parts_far])
    done = swap(payload, "near")

    def widen_kernel(in_ref, gq_ref, gk_ref):
        for h in range(heads):
            for part in range(per_head):
                rows = slice(part * chunk, (part + 1) * chunk)
                gk_ref[h, rows] = in_ref[h * per_head + part, :chunk].astype(F32)
                gq_ref[h, rows] = in_ref[h * per_head + part, chunk:].astype(F32)

    grad_feat_query, grad_feat_key = run(
        widen_kernel, [(feat_query.shape, F32), (feat_key.shape, F32)], [done]
    )
    return (attended, grad_query, grad_key, grad_value, grad_feat_query, grad_feat_key, grad_gain)


def solution(mesh):
    seq, head = mesh.devices.shape
    split = Mesh(mesh.devices.reshape(seq // NEAR, NEAR, head), ("far", "near", "head"))
    wide = P(("far", "near"), "head")
    per_head = P("head", None, None)
    in_specs = (wide, wide, wide, per_head, per_head, P("head"), wide)
    out_specs = (wide, wide, wide, wide, per_head, per_head, P("head"))
    return jax.shard_map(shards, mesh=split, in_specs=in_specs, out_specs=out_specs, check_vma=False)
```

```python
import jax
import jax.numpy as jnp
from jax import lax
from jax.experimental import pallas as pl
from jax.experimental.pallas import tpu as pltpu
from jax.sharding import Mesh, PartitionSpec as P

EPSILON = 1e-05
BF = jnp.bfloat16
F32 = jnp.float32
NEAR = 8
GAIN_ROWS = 16
STAT_ROWS = 8
TOKEN = ((8, 128), F32)
VMEM_BYTES = 24 * 1024 * 1024
WHOLE_VMEM = 64 * 1024 * 1024
MOST_VMEM = 52 * 1024 * 1024


def swap(x, axis):
    return lax.all_to_all(x, axis, 0, 0)


def run(kernel, outs, ins, after=(), fetch=(), limit=VMEM_BYTES):
    count, copies = len(ins), len(fetch)

    def body(*refs):
        sources = refs[count : count + copies]
        outputs = refs[count + copies + len(after) : count + copies + len(after) + len(outs)]
        if not copies:
            return kernel(*refs[:count], *outputs)
        held, sems = refs[-copies - 1 : -1], refs[-1]
        moves = [pltpu.make_async_copy(sources[i], held[i], sems.at[i]) for i in range(copies)]
        for move in moves:
            move.start()
        return kernel(*refs[:count], *held, *outputs, [move.wait for move in moves])

    whole = pl.BlockSpec(memory_space=pltpu.VMEM)
    far_off = pl.BlockSpec(memory_space=pl.ANY)
    scratch = [pltpu.VMEM(x.shape, x.dtype) for x in fetch]
    return pl.pallas_call(
        body,
        out_shape=[jax.ShapeDtypeStruct(shape, dtype) for shape, dtype in outs],
        in_specs=[whole] * count
        + [far_off] * copies
        + [far_off] * len(after),
        out_specs=[whole] * len(outs),
        scratch_shapes=scratch + [pltpu.SemaphoreType.DMA((copies,))] if copies else [],
        compiler_params=pltpu.CompilerParams(vmem_limit_bytes=limit),
        cost_estimate=pl.CostEstimate(flops=10**8, bytes_accessed=10**6, transcendentals=0),
    )(*ins, *fetch, *after)


def dot(a, b, over_a, over_b):
    return lax.dot_general(a, b, (((over_a,), (over_b,)), ((), ())), preferred_element_type=F32)


def silu_slope(x):
    g = 1.0 / (1.0 + jnp.exp(-x))
    return g * (1.0 + x * (1.0 - g))


def causal_mask(count):
    rows = lax.broadcasted_iota(jnp.int32, (count, count), 0)
    cols = lax.broadcasted_iota(jnp.int32, (count, count), 1)
    return rows >= cols


def shards(query_rows, key_rows, value_rows, feat_query, feat_key, norm_gain, grad_out):
    tokens, width = query_rows.shape
    heads, size = feat_query.shape[0], feat_query.shape[1]
    near, far = lax.axis_size("near"), lax.axis_size("far")
    full_width = width * lax.axis_size("head")
    chunk = heads * size // near
    slim = chunk // far
    per_head = near // heads
    gain_row = norm_gain.reshape(1, width)
    place = jnp.stack([lax.axis_index("far"), lax.axis_index("near")])
    group_keys = lax.all_gather(key_rows, "near")
    group_values = lax.all_gather(value_rows, "near")
    cols = [slice(h * size, (h + 1) * size) for h in range(heads)]

    def put_state(out_ref, h, value, row):
        for part in range(per_head):
            rows = value[part * chunk : (part + 1) * chunk]
            out_ref[h * per_head + part, row : row + chunk, :] = rows.astype(BF)

    def get_state(ref, h):
        parts = [ref[h * per_head + part] for part in range(per_head)]
        return jnp.concatenate(parts, axis=0)

    def state_kernel(w_ref, k_ref, v_ref, kf_ref, out_ref, waits):
        waits[0]()
        waits[1]()
        for h, at in enumerate(cols):
            pre = dot(k_ref[:, at], w_ref[h], 1, 0)
            kf_ref[:, at] = (pre / (1.0 + jnp.exp(-pre))).astype(BF)
        waits[2]()
        for h, at in enumerate(cols):
            put_state(out_ref, h, dot(kf_ref[:, at], v_ref[:, at], 0, 0), 0)

    key_feat, payload = run(
        state_kernel,
        [((tokens, width), BF), ((near, chunk, size), BF)],
        [],
        fetch=[feat_key, key_rows, value_rows],
        limit=WHOLE_VMEM,
    )
    parts = swap(payload, "near")

    def query_kernel(kf_ref, wq_ref, q_ref, v_ref, gain_ref, qf_ref, intra_ref, gain_out):
        gain_out[...] = gain_ref[...]
        mask = causal_mask(tokens)
        for h, at in enumerate(cols):
            pre = dot(q_ref[:, at], wq_ref[h], 1, 0)
            feat = (pre / (1.0 + jnp.exp(-pre))).astype(BF)
            qf_ref[:, at] = feat
            scores = jnp.where(mask, dot(feat, kf_ref[:, at], 1, 1), 0.0).astype(BF)
            intra_ref[:, at] = dot(scores, v_ref[:, at], 1, 0)

    query_feat, intra, gain_row = run(
        query_kernel,
        [((tokens, width), BF), ((tokens, width), F32), ((1, width), F32)],
        [key_feat, feat_query, query_rows, value_rows, gain_row],
        after=[place],
    )

    def total_kernel(in_ref, out_ref):
        total = in_ref[0].astype(F32)
        for i in range(1, near):
            total = total + in_ref[i].astype(F32)
        total = total.astype(BF)
        for i in range(out_ref.shape[0]):
            out_ref[i] = total

    (payload,) = run(total_kernel, [((far, chunk, size), BF)], [parts], after=[query_feat])
    parts_far = swap(payload, "far")

    def join(parts_ref, far_ref, place_ref, out_ref, backward):
        place = place_ref[0]
        state = jnp.zeros((chunk, size), F32)
        for i in range(far):
            keep = (i > place) if backward else (i < place)
            state = state + jnp.where(keep, far_ref[i][:chunk].astype(F32), 0.0)
        for i in range(near - 1, -1, -1) if backward else range(near):
            out_ref[i] = state.astype(BF)
            state = state + parts_ref[i][:chunk].astype(F32)

    def run_join(kernel, outs, ins):
        whole = pl.BlockSpec(memory_space=pltpu.VMEM)
        return pl.pallas_call(
            kernel,
            out_shape=[jax.ShapeDtypeStruct(shape, dtype) for shape, dtype in outs],
            in_specs=[whole] * (len(ins) - 1) + [pl.BlockSpec(memory_space=pltpu.SMEM)],
            out_specs=[whole] * len(outs),
            compiler_params=pltpu.CompilerParams(vmem_limit_bytes=VMEM_BYTES),
            cost_estimate=pl.CostEstimate(flops=10**6, bytes_accessed=10**6, transcendentals=0),
        )(*ins)

    def prior_kernel(parts_ref, far_ref, place_ref, out_ref):
        join(parts_ref, far_ref, place_ref, out_ref, False)

    (payload,) = run_join(prior_kernel, [((near, chunk, size), BF)], [parts, parts_far, place])
    prior = swap(payload, "near")

    def norm_kernel(qf_ref, p_ref, intra_ref, go_ref, gain_ref, pre_ref, out_ref):
        squares = jnp.zeros((tokens, size), F32)
        inner = jnp.zeros((tokens, size), F32)
        for h, at in enumerate(cols):
            pre = intra_ref[:, at] + dot(qf_ref[:, at], get_state(p_ref, h), 1, 0)
            pre_ref[:, at] = pre
            squares = squares + pre * pre
            inner = inner + go_ref[:, at].astype(F32) * gain_ref[:, at] * pre
        squares = jnp.sum(squares, axis=1, keepdims=True)
        inner = jnp.sum(inner, axis=1, keepdims=True)
        lane = lax.broadcasted_iota(jnp.int32, (tokens, size), 1)
        both = jnp.where(lane == 0, squares, jnp.where(lane == 1, inner, 0.0))
        rows = jnp.transpose(both)[:STAT_ROWS]
        for i in range(out_ref.shape[0]):
            out_ref[i] = rows

    peers = lax.axis_size("head")
    pre_norm, payload = run(
        norm_kernel,
        [((tokens, width), F32), ((peers, STAT_ROWS, tokens), F32)],
        [query_feat, prior, intra, grad_out, gain_row],
    )
    stats = swap(payload, "head")

    def row_factors(st_ref):
        rows = st_ref[0]
        for i in range(1, peers):
            rows = rows + st_ref[i]
        rows = jnp.concatenate([rows, jnp.zeros((size - STAT_ROWS, tokens), F32)], axis=0)
        both = jnp.transpose(rows)
        inverse = 1.0 / jnp.sqrt(both[:, 0:1] / full_width + EPSILON)
        return inverse, both[:, 1:2] * inverse / full_width

    def delta_of(at, inverse, slope, pre_ref, go_ref, gain_ref):
        normed = pre_ref[:, at] * inverse
        wide = go_ref[:, at].astype(F32)
        return ((wide * gain_ref[:, at] - normed * slope) * inverse).astype(BF), wide, normed

    def query_side(h, at, delta, mask, v_ref, kf_ref, p_ref, q_ref, wq_ref):
        back = jnp.where(mask, dot(delta, v_ref[:, at], 1, 1), 0.0).astype(BF)
        grad = dot(back, kf_ref[:, at], 1, 0) + dot(delta, get_state(p_ref, h), 1, 1)
        return back, (grad * silu_slope(dot(q_ref[:, at], wq_ref[h], 1, 0))).astype(BF)

    def delta_kernel(st_ref, pre_ref, go_ref, gain_ref, qf_ref, v_ref, kf_ref, p_ref, q_ref, wq_ref, k_ref, wk_ref, out_ref):
        inverse, slope = row_factors(st_ref)
        mask = causal_mask(tokens)
        gains = []
        for h, at in enumerate(cols):
            delta, wide, normed = delta_of(at, inverse, slope, pre_ref, go_ref, gain_ref)
            gains.append(jnp.sum(wide * normed, axis=0, keepdims=True))
            put_state(out_ref, h, dot(qf_ref[:, at], delta, 0, 0), 0)
            back, grad = query_side(h, at, delta, mask, v_ref, kf_ref, p_ref, q_ref, wq_ref)
            put_state(out_ref, h, dot(q_ref[:, at], grad, 0, 0), chunk)
            grad = dot(back, qf_ref[:, at], 0, 0) * silu_slope(dot(k_ref[:, at], wk_ref[h], 1, 0))
            put_state(out_ref, h, dot(grad.astype(BF), k_ref[:, at], 0, 0), 2 * chunk)
        rest = [jnp.zeros((GAIN_ROWS - heads, size), F32)]
        rows = jnp.concatenate(gains + rest, axis=0).astype(BF)
        for i in range(near):
            out_ref[i, 3 * chunk :, :] = rows

    (payload,) = run(
        delta_kernel,
        [((near, 3 * chunk + GAIN_ROWS, size), BF)],
        [
            stats, pre_norm, grad_out, gain_row, query_feat, value_rows, key_feat, prior,
            query_rows, feat_query, key_rows, feat_key,
        ],
    )
    parts = swap(payload, "near")

    def local_kernel(
        st_ref, pre_ref, go_ref, gain_ref, qf_ref, v_ref, kf_ref, p_ref, q_ref, wq_ref, k_ref, wk_ref,
        att_ref, gq_ref, kg_ref, ks_ref, gv_ref, token_ref,
    ):
        token_ref[...] = jnp.zeros(token_ref.shape, F32)
        inverse, slope = row_factors(st_ref)
        mask = causal_mask(tokens)
        for h, at in enumerate(cols):
            delta, _, normed = delta_of(at, inverse, slope, pre_ref, go_ref, gain_ref)
            att_ref[:, at] = (normed * gain_ref[:, at]).astype(BF)
            back, grad = query_side(h, at, delta, mask, v_ref, kf_ref, p_ref, q_ref, wq_ref)
            gq_ref[:, at] = dot(grad, wq_ref[h], 1, 1).astype(BF)
            kg_ref[:, at] = dot(back, qf_ref[:, at], 0, 0).astype(BF)
            ks_ref[:, at] = silu_slope(dot(k_ref[:, at], wk_ref[h], 1, 0)).astype(BF)
            scores = jnp.where(mask, dot(qf_ref[:, at], kf_ref[:, at], 1, 1), 0.0).astype(BF)
            gv_ref[:, at] = dot(scores, delta, 0, 0).astype(BF)

    attended, grad_query, key_grad_local, key_slope, grad_value_local, token = run(
        local_kernel,
        [((tokens, width), BF)] * 5 + [TOKEN],
        [
            stats, pre_norm, grad_out, gain_row, query_feat, value_rows, key_feat, prior,
            query_rows, feat_query, key_rows, feat_key,
        ],
    )

    def chunk_kernel(place_ref, wk_ref, keys_ref, values_ref, token_in, k_ref, v_ref, slope_ref, token_ref, sems):
        head = place_ref[1] // per_head
        at = pl.ds(pl.multiple_of(head * size, size), size)
        moves = [
            pltpu.make_async_copy(keys_ref.at[:, :, at], k_ref, sems.at[0]),
            pltpu.make_async_copy(values_ref.at[:, :, at], v_ref, sems.at[1]),
        ]
        for move in moves:
            move.start()
        token_ref[...] = jnp.zeros(token_ref.shape, F32)
        weights = wk_ref[head]
        part = place_ref[1] % per_head
        moves[0].wait()
        for i in range(near):
            slope = silu_slope(dot(k_ref[i], weights, 1, 0))
            mine = slope[:, :chunk]
            for other in range(1, per_head):
                mine = jnp.where(part == other, slope[:, other * chunk : (other + 1) * chunk], mine)
            slope_ref[i] = mine.astype(BF)
        moves[1].wait()

    whole = pl.BlockSpec(memory_space=pltpu.VMEM)
    anywhere = pl.BlockSpec(memory_space=pl.ANY)
    scalars = pl.BlockSpec(memory_space=pltpu.SMEM)
    chunk_keys, chunk_values, chunk_slope, token = pl.pallas_call(
        chunk_kernel,
        out_shape=[
            jax.ShapeDtypeStruct((near, tokens, size), BF),
            jax.ShapeDtypeStruct((near, tokens, size), BF),
            jax.ShapeDtypeStruct((near, tokens, chunk), BF),
            jax.ShapeDtypeStruct(*TOKEN),
        ],
        in_specs=[scalars, whole, anywhere, anywhere, anywhere],
        out_specs=[whole] * 4,
        scratch_shapes=[pltpu.SemaphoreType.DMA((2,))],
        compiler_params=pltpu.CompilerParams(vmem_limit_bytes=MOST_VMEM),
        cost_estimate=pl.CostEstimate(flops=10**8, bytes_accessed=10**6, transcendentals=0),
    )(place, feat_key, group_keys, group_values, token)

    def back_total_kernel(in_ref, out_ref):
        total = in_ref[0].astype(F32)
        for i in range(1, near):
            total = total + in_ref[i].astype(F32)
        head_rows, gains = total[:chunk], total[3 * chunk : 3 * chunk + 8]
        for i in range(far):
            part = total[chunk + i * slim : chunk + (i + 1) * slim]
            out_ref[i] = jnp.concatenate([head_rows, part, gains], axis=0).astype(BF)

    (payload,) = run(
        back_total_kernel, [((far, chunk + slim + 8, size), BF)], [parts], after=[token]
    )
    parts_far = swap(payload, "far")

    def later_kernel(parts_ref, far_ref, k_ref, v_ref, slope_ref, place_ref, out_ref, later_ref, gain_ref):
        join(parts_ref, far_ref, place_ref, later_ref, True)
        side = far_ref[0].astype(F32)[chunk:]
        for i in range(1, far):
            side = side + far_ref[i].astype(F32)[chunk:]
        for h in range(heads):
            gain_ref[h * size : (h + 1) * size] = side[slim + h]
        total = jnp.zeros((chunk, size), F32)
        for i in range(near):
            grad = dot(v_ref[i], later_ref[i], 1, 1) * slope_ref[i].astype(F32)
            total = total + dot(grad.astype(BF), k_ref[i], 0, 0)
            total = total + parts_ref[i].astype(F32)[2 * chunk : 3 * chunk]
        pad = jnp.zeros((8, size), F32)
        total = jnp.concatenate([total, side[:slim], pad], axis=0).astype(BF)
        for i in range(far):
            out_ref[i] = total

    payload, later, grad_gain = run_join(
        later_kernel,
        [((far, chunk + slim + 8, size), BF), ((near, chunk, size), BF), ((width,), F32)],
        [parts, parts_far, chunk_keys, chunk_values, chunk_slope, place],
    )
    parts_far = swap(payload, "far")

    def weight_kernel(far_ref, later_ref, out_ref):
        total = far_ref[0].astype(F32)[:chunk]
        for i in range(1, far):
            total = total + far_ref[i].astype(F32)[:chunk]
        queries = [far_ref[i].astype(F32)[chunk : chunk + slim] for i in range(far)]
        total = jnp.concatenate([total] + queries, axis=0).astype(BF)
        for i in range(near):
            out_ref[i, :chunk] = later_ref[i]
            out_ref[i, chunk:] = total

    (payload,) = run(weight_kernel, [((near, 3 * chunk, size), BF)], [parts_far, later])
    done = swap(payload, "near")

    def last_kernel(
        in_ref, kg_ref, ks_ref, v_ref, wk_ref, gv_ref, kf_ref, gk_ref, gvalue_ref, gfq_ref, gfk_ref
    ):
        for h, at in enumerate(cols):
            mine = range(h * per_head, (h + 1) * per_head)
            later = jnp.concatenate([in_ref[j, :chunk] for j in mine], axis=0)
            grad = kg_ref[:, at].astype(F32) + dot(v_ref[:, at], later, 1, 1)
            grad = (grad * ks_ref[:, at].astype(F32)).astype(BF)
            gk_ref[:, at] = dot(grad, wk_ref[h], 1, 1).astype(BF)
            value = gv_ref[:, at].astype(F32) + dot(kf_ref[:, at], later, 1, 0)
            gvalue_ref[:, at] = value.astype(BF)
            rows = [in_ref[j, chunk : 2 * chunk].astype(F32) for j in mine]
            gfk_ref[h] = jnp.transpose(jnp.concatenate(rows, axis=0))
            rows = [in_ref[j, 2 * chunk :].astype(F32) for j in mine]
            gfq_ref[h] = jnp.concatenate(rows, axis=0)

    grad_key, grad_value, grad_feat_query, grad_feat_key = run(
        last_kernel,
        [((tokens, width), BF), ((tokens, width), BF), (feat_query.shape, F32), (feat_key.shape, F32)],
        [done, key_grad_local, key_slope, value_rows, feat_key, grad_value_local, key_feat],
    )
    return (attended, grad_query, grad_key, grad_value, grad_feat_query, grad_feat_key, grad_gain)


def solution(mesh):
    seq, head = mesh.devices.shape
    split = Mesh(mesh.devices.reshape(seq // NEAR, NEAR, head), ("far", "near", "head"))
    wide = P(("far", "near"), "head")
    per_head = P("head", None, None)
    in_specs = (wide, wide, wide, per_head, per_head, P("head"), wide)
    out_specs = (wide, wide, wide, wide, per_head, per_head, P("head"))
    return jax.shard_map(shards, mesh=split, in_specs=in_specs, out_specs=out_specs, check_vma=False)
```

```python
import math

import jax
import jax.numpy as jnp
from jax import lax
from jax.experimental import pallas as pl
from jax.experimental.pallas import tpu as pltpu
from jax.sharding import Mesh, PartitionSpec as P

EPSILON = 1e-05
BF = jnp.bfloat16
F32 = jnp.float32
NEAR = ("row", "pair", "side")
GAIN_ROWS = 16
STAT_ROWS = 8
TOKEN = ((8, 128), F32)
VMEM_BYTES = 24 * 1024 * 1024
WHOLE_VMEM = 64 * 1024 * 1024
MOST_VMEM = 52 * 1024 * 1024


def swap(x, axis):
    return lax.all_to_all(x, axis, 0, 0)


def run(kernel, outs, ins, after=(), fetch=(), limit=VMEM_BYTES):
    count, copies = len(ins), len(fetch)

    def body(*refs):
        sources = refs[count : count + copies]
        outputs = refs[count + copies + len(after) : count + copies + len(after) + len(outs)]
        if not copies:
            return kernel(*refs[:count], *outputs)
        held, sems = refs[-copies - 1 : -1], refs[-1]
        moves = [pltpu.make_async_copy(sources[i], held[i], sems.at[i]) for i in range(copies)]
        for move in moves:
            move.start()
        return kernel(*refs[:count], *held, *outputs, [move.wait for move in moves])

    whole = pl.BlockSpec(memory_space=pltpu.VMEM)
    far_off = pl.BlockSpec(memory_space=pl.ANY)
    scratch = [pltpu.VMEM(x.shape, x.dtype) for x in fetch]
    return pl.pallas_call(
        body,
        out_shape=[jax.ShapeDtypeStruct(shape, dtype) for shape, dtype in outs],
        in_specs=[whole] * count
        + [far_off] * copies
        + [far_off] * len(after),
        out_specs=[whole] * len(outs),
        scratch_shapes=scratch + [pltpu.SemaphoreType.DMA((copies,))] if copies else [],
        compiler_params=pltpu.CompilerParams(vmem_limit_bytes=limit),
        cost_estimate=pl.CostEstimate(flops=10**8, bytes_accessed=10**6, transcendentals=0),
    )(*ins, *fetch, *after)


def dot(a, b, over_a, over_b):
    return lax.dot_general(a, b, (((over_a,), (over_b,)), ((), ())), preferred_element_type=F32)


def silu_slope(x):
    g = 1.0 / (1.0 + jnp.exp(-x))
    return g * (1.0 + x * (1.0 - g))


def causal_mask(count):
    rows = lax.broadcasted_iota(jnp.int32, (count, count), 0)
    cols = lax.broadcasted_iota(jnp.int32, (count, count), 1)
    return rows >= cols


def shards(query_rows, key_rows, value_rows, feat_query, feat_key, norm_gain, grad_out):
    tokens, width = query_rows.shape
    heads, size = feat_query.shape[0], feat_query.shape[1]
    near, far = math.prod(lax.axis_size(name) for name in NEAR), lax.axis_size("far")
    full_width = width * lax.axis_size("head")
    chunk = heads * size // near
    slim = chunk // far
    per_head = near // heads
    gain_row = norm_gain.reshape(1, width)
    place = jnp.stack([lax.axis_index("far"), lax.axis_index(NEAR)])
    cols = [slice(h * size, (h + 1) * size) for h in range(heads)]

    def put_state(out_ref, h, value, row):
        for part in range(per_head):
            rows = value[part * chunk : (part + 1) * chunk]
            out_ref[h * per_head + part, row : row + chunk, :] = rows.astype(BF)

    def get_state(ref, h):
        parts = [ref[h * per_head + part] for part in range(per_head)]
        return jnp.concatenate(parts, axis=0)

    def state_kernel(w_ref, k_ref, v_ref, kf_ref, out_ref, both_ref, waits):
        waits[0]()
        waits[1]()
        for h, at in enumerate(cols):
            pre = dot(k_ref[:, at], w_ref[h], 1, 0)
            kf_ref[:, at] = (pre / (1.0 + jnp.exp(-pre))).astype(BF)
        both_ref[:, :width] = k_ref[...]
        waits[2]()
        both_ref[:, width:] = v_ref[...]
        for h, at in enumerate(cols):
            put_state(out_ref, h, dot(kf_ref[:, at], v_ref[:, at], 0, 0), 0)

    key_feat, payload, both = run(
        state_kernel,
        [((tokens, width), BF), ((near, chunk, size), BF), ((tokens, 2 * width), BF)],
        [],
        fetch=[feat_key, key_rows, value_rows],
        limit=WHOLE_VMEM,
    )
    gathered = lax.all_gather(both, NEAR[:2])
    parts = swap(payload, NEAR)

    def query_kernel(kf_ref, wq_ref, q_ref, v_ref, gain_ref, qf_ref, intra_ref, gain_out):
        gain_out[...] = gain_ref[...]
        mask = causal_mask(tokens)
        for h, at in enumerate(cols):
            pre = dot(q_ref[:, at], wq_ref[h], 1, 0)
            feat = (pre / (1.0 + jnp.exp(-pre))).astype(BF)
            qf_ref[:, at] = feat
            scores = jnp.where(mask, dot(feat, kf_ref[:, at], 1, 1), 0.0).astype(BF)
            intra_ref[:, at] = dot(scores, v_ref[:, at], 1, 0)

    query_feat, intra, gain_row = run(
        query_kernel,
        [((tokens, width), BF), ((tokens, width), F32), ((1, width), F32)],
        [key_feat, feat_query, query_rows, value_rows, gain_row],
        after=[place],
    )

    def total_kernel(in_ref, out_ref):
        total = in_ref[0].astype(F32)
        for i in range(1, near):
            total = total + in_ref[i].astype(F32)
        total = total.astype(BF)
        for i in range(out_ref.shape[0]):
            out_ref[i] = total

    (payload,) = run(total_kernel, [((far, chunk, size), BF)], [parts], after=[query_feat])
    parts_far = swap(payload, "far")

    def join(parts_ref, far_ref, place_ref, out_ref, backward):
        place = place_ref[0]
        state = jnp.zeros((chunk, size), F32)
        for i in range(far):
            keep = (i > place) if backward else (i < place)
            state = state + jnp.where(keep, far_ref[i][:chunk].astype(F32), 0.0)
        for i in range(near - 1, -1, -1) if backward else range(near):
            out_ref[i] = state.astype(BF)
            state = state + parts_ref[i][:chunk].astype(F32)

    def run_join(kernel, outs, ins):
        whole = pl.BlockSpec(memory_space=pltpu.VMEM)
        return pl.pallas_call(
            kernel,
            out_shape=[jax.ShapeDtypeStruct(shape, dtype) for shape, dtype in outs],
            in_specs=[whole] * (len(ins) - 1) + [pl.BlockSpec(memory_space=pltpu.SMEM)],
            out_specs=[whole] * len(outs),
            compiler_params=pltpu.CompilerParams(vmem_limit_bytes=VMEM_BYTES),
            cost_estimate=pl.CostEstimate(flops=10**6, bytes_accessed=10**6, transcendentals=0),
        )(*ins)

    def prior_kernel(parts_ref, far_ref, place_ref, out_ref):
        join(parts_ref, far_ref, place_ref, out_ref, False)

    (payload,) = run_join(prior_kernel, [((near, chunk, size), BF)], [parts, parts_far, place])
    prior = swap(payload, NEAR)

    def norm_kernel(qf_ref, p_ref, intra_ref, go_ref, gain_ref, pre_ref, out_ref):
        squares = jnp.zeros((tokens, size), F32)
        inner = jnp.zeros((tokens, size), F32)
        for h, at in enumerate(cols):
            pre = intra_ref[:, at] + dot(qf_ref[:, at], get_state(p_ref, h), 1, 0)
            pre_ref[:, at] = pre
            squares = squares + pre * pre
            inner = inner + go_ref[:, at].astype(F32) * gain_ref[:, at] * pre
        squares = jnp.sum(squares, axis=1, keepdims=True)
        inner = jnp.sum(inner, axis=1, keepdims=True)
        lane = lax.broadcasted_iota(jnp.int32, (tokens, size), 1)
        both = jnp.where(lane == 0, squares, jnp.where(lane == 1, inner, 0.0))
        rows = jnp.transpose(both)[:STAT_ROWS]
        for i in range(out_ref.shape[0]):
            out_ref[i] = rows

    peers = lax.axis_size("head")
    pre_norm, payload = run(
        norm_kernel,
        [((tokens, width), F32), ((peers, STAT_ROWS, tokens), F32)],
        [query_feat, prior, intra, grad_out, gain_row],
    )
    stats = swap(payload, "head")

    def row_factors(st_ref):
        rows = st_ref[0]
        for i in range(1, peers):
            rows = rows + st_ref[i]
        rows = jnp.concatenate([rows, jnp.zeros((size - STAT_ROWS, tokens), F32)], axis=0)
        both = jnp.transpose(rows)
        inverse = 1.0 / jnp.sqrt(both[:, 0:1] / full_width + EPSILON)
        return inverse, both[:, 1:2] * inverse / full_width

    def delta_of(at, inverse, slope, pre_ref, go_ref, gain_ref):
        normed = pre_ref[:, at] * inverse
        wide = go_ref[:, at].astype(F32)
        return ((wide * gain_ref[:, at] - normed * slope) * inverse).astype(BF), wide, normed

    def query_side(h, at, delta, mask, v_ref, kf_ref, p_ref, q_ref, wq_ref):
        back = jnp.where(mask, dot(delta, v_ref[:, at], 1, 1), 0.0).astype(BF)
        grad = dot(back, kf_ref[:, at], 1, 0) + dot(delta, get_state(p_ref, h), 1, 1)
        return back, (grad * silu_slope(dot(q_ref[:, at], wq_ref[h], 1, 0))).astype(BF)

    def delta_kernel(st_ref, pre_ref, go_ref, gain_ref, qf_ref, v_ref, kf_ref, p_ref, q_ref, wq_ref, k_ref, wk_ref, out_ref):
        inverse, slope = row_factors(st_ref)
        mask = causal_mask(tokens)
        gains = []
        for h, at in enumerate(cols):
            delta, wide, normed = delta_of(at, inverse, slope, pre_ref, go_ref, gain_ref)
            gains.append(jnp.sum(wide * normed, axis=0, keepdims=True))
            put_state(out_ref, h, dot(qf_ref[:, at], delta, 0, 0), 0)
            back, grad = query_side(h, at, delta, mask, v_ref, kf_ref, p_ref, q_ref, wq_ref)
            put_state(out_ref, h, dot(q_ref[:, at], grad, 0, 0), chunk)
            grad = dot(back, qf_ref[:, at], 0, 0) * silu_slope(dot(k_ref[:, at], wk_ref[h], 1, 0))
            put_state(out_ref, h, dot(grad.astype(BF), k_ref[:, at], 0, 0), 2 * chunk)
        rest = [jnp.zeros((GAIN_ROWS - heads, size), F32)]
        rows = jnp.concatenate(gains + rest, axis=0).astype(BF)
        for i in range(near):
            out_ref[i, 3 * chunk :, :] = rows

    (payload,) = run(
        delta_kernel,
        [((near, 3 * chunk + GAIN_ROWS, size), BF)],
        [
            stats, pre_norm, grad_out, gain_row, query_feat, value_rows, key_feat, prior,
            query_rows, feat_query, key_rows, feat_key,
        ],
    )
    parts = swap(payload, NEAR)

    def local_kernel(
        st_ref, pre_ref, go_ref, gain_ref, qf_ref, v_ref, kf_ref, p_ref, q_ref, wq_ref, k_ref, wk_ref,
        att_ref, gq_ref, kg_ref, ks_ref, gv_ref, token_ref,
    ):
        token_ref[...] = jnp.zeros(token_ref.shape, F32)
        inverse, slope = row_factors(st_ref)
        mask = causal_mask(tokens)
        for h, at in enumerate(cols):
            delta, _, normed = delta_of(at, inverse, slope, pre_ref, go_ref, gain_ref)
            att_ref[:, at] = (normed * gain_ref[:, at]).astype(BF)
            back, grad = query_side(h, at, delta, mask, v_ref, kf_ref, p_ref, q_ref, wq_ref)
            gq_ref[:, at] = dot(grad, wq_ref[h], 1, 1).astype(BF)
            kg_ref[:, at] = dot(back, qf_ref[:, at], 0, 0).astype(BF)
            ks_ref[:, at] = silu_slope(dot(k_ref[:, at], wk_ref[h], 1, 0)).astype(BF)
            scores = jnp.where(mask, dot(qf_ref[:, at], kf_ref[:, at], 1, 1), 0.0).astype(BF)
            gv_ref[:, at] = dot(scores, delta, 0, 0).astype(BF)

    attended, grad_query, key_grad_local, key_slope, grad_value_local, token = run(
        local_kernel,
        [((tokens, width), BF)] * 5 + [TOKEN],
        [
            stats, pre_norm, grad_out, gain_row, query_feat, value_rows, key_feat, prior,
            query_rows, feat_query, key_rows, feat_key,
        ],
    )

    def pick_kernel(place_ref, both_ref, token_in, out_ref, token_ref, sems):
        moves = []
        for i in range(2):
            at = pl.multiple_of(place_ref[1] // per_head * size + i * width, size)
            source = both_ref.at[:, :, pl.ds(at, size)]
            moves.append(pltpu.make_async_copy(source, out_ref.at[i], sems.at[i]))
        for move in moves:
            move.start()
        token_ref[...] = jnp.zeros(token_ref.shape, F32)
        for move in moves:
            move.wait()

    whole = pl.BlockSpec(memory_space=pltpu.VMEM)
    anywhere = pl.BlockSpec(memory_space=pl.ANY)
    scalars = pl.BlockSpec(memory_space=pltpu.SMEM)
    picked, token = pl.pallas_call(
        pick_kernel,
        out_shape=[
            jax.ShapeDtypeStruct((2, near // per_head, tokens, size), BF),
            jax.ShapeDtypeStruct(*TOKEN),
        ],
        in_specs=[scalars, anywhere, anywhere],
        out_specs=[whole] * 2,
        scratch_shapes=[pltpu.SemaphoreType.DMA((2,))],
        compiler_params=pltpu.CompilerParams(vmem_limit_bytes=MOST_VMEM),
        cost_estimate=pl.CostEstimate(flops=10**8, bytes_accessed=10**6, transcendentals=0),
    )(place, gathered, token)
    other = lax.ppermute(picked, NEAR[2], [(0, 1), (1, 0)])

    def back_total_kernel(in_ref, out_ref):
        total = in_ref[0].astype(F32)
        for i in range(1, near):
            total = total + in_ref[i].astype(F32)
        head_rows, gains = total[:chunk], total[3 * chunk : 3 * chunk + 8]
        for i in range(far):
            part = total[chunk + i * slim : chunk + (i + 1) * slim]
            out_ref[i] = jnp.concatenate([head_rows, part, gains], axis=0).astype(BF)

    (payload,) = run(
        back_total_kernel, [((far, chunk + slim + 8, size), BF)], [parts], after=[token]
    )
    parts_far = swap(payload, "far")

    def later_kernel(parts_ref, far_ref, own_ref, other_ref, wk_ref, place_ref, out_ref, later_ref, gain_ref):
        join(parts_ref, far_ref, place_ref, later_ref, True)
        side = far_ref[0].astype(F32)[chunk:]
        for i in range(1, far):
            side = side + far_ref[i].astype(F32)[chunk:]
        for h in range(heads):
            gain_ref[h * size : (h + 1) * size] = side[slim + h]
        total = jnp.zeros((chunk, size), F32)
        part = place_ref[1] % per_head
        weights = wk_ref[place_ref[1] // per_head]
        weights = jnp.where(part == 0, weights[:, :chunk], weights[:, chunk:])
        for i in range(near // per_head):
            for ref, offset in ((own_ref, part), (other_ref, 1 - part)):
                keys = ref[0, i]
                grad = dot(ref[1, i], later_ref[per_head * i + offset], 1, 1)
                grad = grad * silu_slope(dot(keys, weights, 1, 0))
                total = total + dot(grad.astype(BF), keys, 0, 0)
        for i in range(near):
            total = total + parts_ref[i].astype(F32)[2 * chunk : 3 * chunk]
        pad = jnp.zeros((8, size), F32)
        total = jnp.concatenate([total, side[:slim], pad], axis=0).astype(BF)
        for i in range(far):
            out_ref[i] = total

    payload, later, grad_gain = run_join(
        later_kernel,
        [((far, chunk + slim + 8, size), BF), ((near, chunk, size), BF), ((width,), F32)],
        [parts, parts_far, picked, other, feat_key, place],
    )
    parts_far = swap(payload, "far")

    def weight_kernel(far_ref, later_ref, out_ref):
        total = far_ref[0].astype(F32)[:chunk]
        for i in range(1, far):
            total = total + far_ref[i].astype(F32)[:chunk]
        queries = [far_ref[i].astype(F32)[chunk : chunk + slim] for i in range(far)]
        total = jnp.concatenate([total] + queries, axis=0).astype(BF)
        for i in range(near):
            out_ref[i, :chunk] = later_ref[i]
            out_ref[i, chunk:] = total

    (payload,) = run(weight_kernel, [((near, 3 * chunk, size), BF)], [parts_far, later])
    done = swap(payload, NEAR)

    def last_kernel(
        in_ref, kg_ref, ks_ref, v_ref, wk_ref, gv_ref, kf_ref, gk_ref, gvalue_ref, gfq_ref, gfk_ref
    ):
        for h, at in enumerate(cols):
            mine = range(h * per_head, (h + 1) * per_head)
            later = jnp.concatenate([in_ref[j, :chunk] for j in mine], axis=0)
            grad = kg_ref[:, at].astype(F32) + dot(v_ref[:, at], later, 1, 1)
            grad = (grad * ks_ref[:, at].astype(F32)).astype(BF)
            gk_ref[:, at] = dot(grad, wk_ref[h], 1, 1).astype(BF)
            value = gv_ref[:, at].astype(F32) + dot(kf_ref[:, at], later, 1, 0)
            gvalue_ref[:, at] = value.astype(BF)
            rows = [in_ref[j, chunk : 2 * chunk].astype(F32) for j in mine]
            gfk_ref[h] = jnp.transpose(jnp.concatenate(rows, axis=0))
            rows = [in_ref[j, 2 * chunk :].astype(F32) for j in mine]
            gfq_ref[h] = jnp.concatenate(rows, axis=0)

    grad_key, grad_value, grad_feat_query, grad_feat_key = run(
        last_kernel,
        [((tokens, width), BF), ((tokens, width), BF), (feat_query.shape, F32), (feat_key.shape, F32)],
        [done, key_grad_local, key_slope, value_rows, feat_key, grad_value_local, key_feat],
    )
    return (attended, grad_query, grad_key, grad_value, grad_feat_query, grad_feat_key, grad_gain)


def solution(mesh):
    seq, head = mesh.devices.shape
    split = Mesh(mesh.devices.reshape(seq // 8, 2, 2, 2, head), ("far",) + NEAR + ("head",))
    wide = P(("far",) + NEAR, "head")
    per_head = P("head", None, None)
    in_specs = (wide, wide, wide, per_head, per_head, P("head"), wide)
    out_specs = (wide, wide, wide, wide, per_head, per_head, P("head"))
    return jax.shard_map(shards, mesh=split, in_specs=in_specs, out_specs=out_specs, check_vma=False)
```

```python
import jax
import jax.numpy as jnp
from jax import lax
from jax.experimental import pallas as pl
from jax.experimental.pallas import tpu as pltpu
from jax.sharding import Mesh, PartitionSpec as P

EPSILON = 1e-05
BF = jnp.bfloat16
F32 = jnp.float32
NEAR = 8
GAIN_ROWS = 16
STAT_ROWS = 8
TOKEN = ((8, 128), F32)
VMEM_BYTES = 24 * 1024 * 1024
WHOLE_VMEM = 64 * 1024 * 1024
STATE_VMEM = 63 * 1024 * 1024


def swap(x, axis):
    return lax.all_to_all(x, axis, 0, 0)


def run(kernel, outs, ins, after=(), fetch=(), limit=VMEM_BYTES):
    count, copies = len(ins), len(fetch)

    def body(*refs):
        sources = refs[count : count + copies]
        outputs = refs[count + copies + len(after) : count + copies + len(after) + len(outs)]
        if not copies:
            return kernel(*refs[:count], *outputs)
        held, sems = refs[-copies - 1 : -1], refs[-1]
        moves = [pltpu.make_async_copy(sources[i], held[i], sems.at[i]) for i in range(copies)]
        for move in moves:
            move.start()
        return kernel(*refs[:count], *held, *outputs, [move.wait for move in moves])

    whole = pl.BlockSpec(memory_space=pltpu.VMEM)
    far_off = pl.BlockSpec(memory_space=pl.ANY)
    scratch = [pltpu.VMEM(x.shape, x.dtype) for x in fetch]
    return pl.pallas_call(
        body,
        out_shape=[jax.ShapeDtypeStruct(shape, dtype) for shape, dtype in outs],
        in_specs=[whole] * count
        + [far_off] * copies
        + [far_off] * len(after),
        out_specs=[whole] * len(outs),
        scratch_shapes=scratch + [pltpu.SemaphoreType.DMA((copies,))] if copies else [],
        compiler_params=pltpu.CompilerParams(vmem_limit_bytes=limit),
        cost_estimate=pl.CostEstimate(flops=10**8, bytes_accessed=10**6, transcendentals=0),
    )(*ins, *fetch, *after)


def dot(a, b, over_a, over_b):
    return lax.dot_general(a, b, (((over_a,), (over_b,)), ((), ())), preferred_element_type=F32)


def silu_slope(x):
    g = 1.0 / (1.0 + jnp.exp(-x))
    return g * (1.0 + x * (1.0 - g))


def causal_mask(count):
    rows = lax.broadcasted_iota(jnp.int32, (count, count), 0)
    cols = lax.broadcasted_iota(jnp.int32, (count, count), 1)
    return rows >= cols


def shards(query_rows, key_rows, value_rows, feat_query, feat_key, norm_gain, grad_out):
    tokens, width = query_rows.shape
    heads, size = feat_query.shape[0], feat_query.shape[1]
    near, far = lax.axis_size("near"), lax.axis_size("far")
    full_width = width * lax.axis_size("head")
    chunk = heads * size // near
    slim = chunk // far
    per_head = near // heads
    gain_row = norm_gain.reshape(1, width)
    cols = [slice(h * size, (h + 1) * size) for h in range(heads)]

    def put_state(out_ref, h, value, row):
        for part in range(per_head):
            rows = value[part * chunk : (part + 1) * chunk]
            out_ref[h * per_head + part, row : row + chunk, :] = rows.astype(BF)

    def get_state(ref, h):
        parts = [ref[h * per_head + part] for part in range(per_head)]
        return jnp.concatenate(parts, axis=0)

    def pack_kernel(k_ref, v_ref, out_ref, held_ref, in_sems, out_sems):
        loads, stores = [], []
        for h, at in enumerate(cols):
            for i, ref in enumerate((k_ref, v_ref)):
                room = held_ref.at[h, pl.ds(i * tokens, tokens), :]
                loads.append(pltpu.make_async_copy(ref.at[:, at], room, in_sems.at[2 * h + i]))
        for load in loads:
            load.start()
        for h in range(heads):
            loads[2 * h].wait()
            loads[2 * h + 1].wait()
            for part in range(per_head):
                place = h * per_head + part
                store = pltpu.make_async_copy(held_ref.at[h], out_ref.at[place], out_sems.at[place])
                store.start()
                stores.append(store)
        for store in stores:
            store.wait()

    whole = pl.BlockSpec(memory_space=pltpu.VMEM)
    anywhere = pl.BlockSpec(memory_space=pl.ANY)
    payload = pl.pallas_call(
        pack_kernel,
        out_shape=jax.ShapeDtypeStruct((near, 2 * tokens, size), BF),
        in_specs=[anywhere, anywhere],
        out_specs=anywhere,
        scratch_shapes=[
            pltpu.VMEM((heads, 2 * tokens, size), BF),
            pltpu.SemaphoreType.DMA((2 * heads,)),
            pltpu.SemaphoreType.DMA((near,)),
        ],
        compiler_params=pltpu.CompilerParams(vmem_limit_bytes=WHOLE_VMEM),
        cost_estimate=pl.CostEstimate(flops=10**6, bytes_accessed=10**6, transcendentals=0),
    )(key_rows, value_rows)
    group_rows = swap(payload, "near")

    def feature_kernel(k_ref, wk_ref, q_ref, wq_ref, kf_ref, qf_ref):
        for h, at in enumerate(cols):
            pre = dot(k_ref[:, at], wk_ref[h], 1, 0)
            kf_ref[:, at] = (pre / (1.0 + jnp.exp(-pre))).astype(BF)
            pre = dot(q_ref[:, at], wq_ref[h], 1, 0)
            qf_ref[:, at] = (pre / (1.0 + jnp.exp(-pre))).astype(BF)

    key_feat, query_feat = run(
        feature_kernel,
        [((tokens, width), BF), ((tokens, width), BF)],
        [key_rows, feat_key, query_rows, feat_query],
    )

    def chunk_weights(wk_ref):
        member = lax.axis_index("near")
        weights = wk_ref[member // per_head]
        part = member % per_head
        mine = weights[:, :chunk]
        for other in range(1, per_head):
            mine = jnp.where(part == other, weights[:, other * chunk : (other + 1) * chunk], mine)
        return mine

    def state_kernel(
        rows_ref, wk_ref, token_ref, parts_ref, slope_ref, out_ref, held_ref, wk_held, sems
    ):
        loads = [pltpu.make_async_copy(wk_ref, wk_held, sems.at[near])]
        for i in range(near):
            loads.append(pltpu.make_async_copy(rows_ref.at[i], held_ref.at[i], sems.at[i]))
        for load in loads:
            load.start()
        loads[0].wait()
        weights = chunk_weights(wk_held)
        total = jnp.zeros((chunk, size), F32)
        for i in range(near):
            loads[i + 1].wait()
            pre = dot(held_ref[i, :tokens], weights, 1, 0)
            gate = 1.0 / (1.0 + jnp.exp(-pre))
            slope_ref[i] = (gate * (1.0 + pre * (1.0 - gate))).astype(BF)
            state = dot((pre * gate).astype(BF), held_ref[i, tokens:], 0, 0)
            parts_ref[i] = state.astype(BF)
            total = total + state
        total = total.astype(BF)
        for i in range(far):
            out_ref[i] = total

    parts, chunk_slope, payload = pl.pallas_call(
        state_kernel,
        out_shape=[
            jax.ShapeDtypeStruct((near, chunk, size), BF),
            jax.ShapeDtypeStruct((near, tokens, chunk), BF),
            jax.ShapeDtypeStruct((far, chunk, size), BF),
        ],
        in_specs=[anywhere, anywhere, anywhere],
        out_specs=[whole] * 3,
        scratch_shapes=[
            pltpu.VMEM((near, 2 * tokens, size), BF),
            pltpu.VMEM(feat_key.shape, BF),
            pltpu.SemaphoreType.DMA((near + 1,)),
        ],
        compiler_params=pltpu.CompilerParams(vmem_limit_bytes=STATE_VMEM),
        cost_estimate=pl.CostEstimate(flops=10**8, bytes_accessed=10**6, transcendentals=0),
    )(group_rows, feat_key, query_feat)
    parts_far = swap(payload, "far")

    def join(parts_ref, far_ref, out_ref, backward):
        place = lax.axis_index("far")
        state = jnp.zeros((chunk, size), F32)
        for i in range(far):
            keep = (i > place) if backward else (i < place)
            state = state + jnp.where(keep, far_ref[i][:chunk].astype(F32), 0.0)
        for i in range(near - 1, -1, -1) if backward else range(near):
            out_ref[i] = state.astype(BF)
            state = state + parts_ref[i][:chunk].astype(F32)

    def prior_kernel(parts_ref, far_ref, out_ref):
        join(parts_ref, far_ref, out_ref, False)

    (payload,) = run(prior_kernel, [((near, chunk, size), BF)], [parts, parts_far])
    prior = swap(payload, "near")

    def norm_kernel(qf_ref, kf_ref, v_ref, p_ref, go_ref, gain_ref, pre_ref, gain_out, out_ref, waits):
        mask = causal_mask(tokens)
        squares = jnp.zeros((tokens, size), F32)
        inner = jnp.zeros((tokens, size), F32)
        for h, at in enumerate(cols):
            scores = jnp.where(mask, dot(qf_ref[:, at], kf_ref[:, at], 1, 1), 0.0).astype(BF)
            pre = dot(scores, v_ref[:, at], 1, 0) + dot(qf_ref[:, at], get_state(p_ref, h), 1, 0)
            pre_ref[:, at] = pre
            squares = squares + pre * pre
            if h == 0:
                waits[0]()
            inner = inner + go_ref[:, at].astype(F32) * gain_ref[:, at] * pre
        gain_out[...] = gain_ref[...]
        squares = jnp.sum(squares, axis=1, keepdims=True)
        inner = jnp.sum(inner, axis=1, keepdims=True)
        lane = lax.broadcasted_iota(jnp.int32, (tokens, size), 1)
        both = jnp.where(lane == 0, squares, jnp.where(lane == 1, inner, 0.0))
        rows = jnp.transpose(both)[:STAT_ROWS]
        for i in range(out_ref.shape[0]):
            out_ref[i] = rows

    peers = lax.axis_size("head")
    pre_norm, gain_row, payload = run(
        norm_kernel,
        [((tokens, width), F32), ((1, width), F32), ((peers, STAT_ROWS, tokens), F32)],
        [query_feat, key_feat, value_rows, prior, grad_out],
        fetch=[gain_row],
    )
    stats = swap(payload, "head")

    def row_factors(st_ref):
        rows = st_ref[0]
        for i in range(1, peers):
            rows = rows + st_ref[i]
        rows = jnp.concatenate([rows, jnp.zeros((size - STAT_ROWS, tokens), F32)], axis=0)
        both = jnp.transpose(rows)
        inverse = 1.0 / jnp.sqrt(both[:, 0:1] / full_width + EPSILON)
        return inverse, both[:, 1:2] * inverse / full_width

    def delta_of(at, inverse, slope, pre_ref, go_ref, gain_ref):
        normed = pre_ref[:, at] * inverse
        wide = go_ref[:, at].astype(F32)
        return ((wide * gain_ref[:, at] - normed * slope) * inverse).astype(BF), wide, normed

    def query_side(h, at, delta, mask, v_ref, kf_ref, p_ref, q_ref, wq_ref):
        back = jnp.where(mask, dot(delta, v_ref[:, at], 1, 1), 0.0).astype(BF)
        grad = dot(back, kf_ref[:, at], 1, 0) + dot(delta, get_state(p_ref, h), 1, 1)
        return back, (grad * silu_slope(dot(q_ref[:, at], wq_ref[h], 1, 0))).astype(BF)

    def delta_kernel(st_ref, pre_ref, go_ref, gain_ref, qf_ref, v_ref, kf_ref, p_ref, q_ref, wq_ref, k_ref, wk_ref, out_ref):
        inverse, slope = row_factors(st_ref)
        mask = causal_mask(tokens)
        gains = []
        for h, at in enumerate(cols):
            delta, wide, normed = delta_of(at, inverse, slope, pre_ref, go_ref, gain_ref)
            gains.append(jnp.sum(wide * normed, axis=0, keepdims=True))
            put_state(out_ref, h, dot(qf_ref[:, at], delta, 0, 0), 0)
            back, grad = query_side(h, at, delta, mask, v_ref, kf_ref, p_ref, q_ref, wq_ref)
            put_state(out_ref, h, dot(q_ref[:, at], grad, 0, 0), chunk)
            grad = dot(back, qf_ref[:, at], 0, 0) * silu_slope(dot(k_ref[:, at], wk_ref[h], 1, 0))
            put_state(out_ref, h, dot(grad.astype(BF), k_ref[:, at], 0, 0), 2 * chunk)
        rest = [jnp.zeros((GAIN_ROWS - heads, size), F32)]
        rows = jnp.concatenate(gains + rest, axis=0).astype(BF)
        for i in range(near):
            out_ref[i, 3 * chunk :, :] = rows

    (payload,) = run(
        delta_kernel,
        [((near, 3 * chunk + GAIN_ROWS, size), BF)],
        [
            stats, pre_norm, grad_out, gain_row, query_feat, value_rows, key_feat, prior,
            query_rows, feat_query, key_rows, feat_key,
        ],
    )
    parts = swap(payload, "near")

    def local_kernel(
        st_ref, pre_ref, go_ref, gain_ref, qf_ref, v_ref, kf_ref, p_ref, q_ref, wq_ref, k_ref, wk_ref,
        att_ref, gq_ref, kg_ref, ks_ref, gv_ref, token_ref,
    ):
        token_ref[...] = jnp.zeros(token_ref.shape, F32)
        inverse, slope = row_factors(st_ref)
        mask = causal_mask(tokens)
        for h, at in enumerate(cols):
            delta, _, normed = delta_of(at, inverse, slope, pre_ref, go_ref, gain_ref)
            att_ref[:, at] = (normed * gain_ref[:, at]).astype(BF)
            back, grad = query_side(h, at, delta, mask, v_ref, kf_ref, p_ref, q_ref, wq_ref)
            gq_ref[:, at] = dot(grad, wq_ref[h], 1, 1).astype(BF)
            kg_ref[:, at] = dot(back, qf_ref[:, at], 0, 0).astype(BF)
            ks_ref[:, at] = silu_slope(dot(k_ref[:, at], wk_ref[h], 1, 0)).astype(BF)
            scores = jnp.where(mask, dot(qf_ref[:, at], kf_ref[:, at], 1, 1), 0.0).astype(BF)
            gv_ref[:, at] = dot(scores, delta, 0, 0).astype(BF)

    attended, grad_query, key_grad_local, key_slope, grad_value_local, token = run(
        local_kernel,
        [((tokens, width), BF)] * 5 + [TOKEN],
        [
            stats, pre_norm, grad_out, gain_row, query_feat, value_rows, key_feat, prior,
            query_rows, feat_query, key_rows, feat_key,
        ],
    )

    def back_total_kernel(in_ref, out_ref):
        total = in_ref[0].astype(F32)
        for i in range(1, near):
            total = total + in_ref[i].astype(F32)
        head_rows, gains = total[:chunk], total[3 * chunk : 3 * chunk + 8]
        for i in range(far):
            part = total[chunk + i * slim : chunk + (i + 1) * slim]
            out_ref[i] = jnp.concatenate([head_rows, part, gains], axis=0).astype(BF)

    (payload,) = run(
        back_total_kernel, [((far, chunk + slim + 8, size), BF)], [parts], after=[token]
    )
    parts_far = swap(payload, "far")

    def later_kernel(parts_ref, far_ref, rows_ref, slope_ref, out_ref, later_ref, gain_ref):
        join(parts_ref, far_ref, later_ref, True)
        side = far_ref[0].astype(F32)[chunk:]
        for i in range(1, far):
            side = side + far_ref[i].astype(F32)[chunk:]
        for h in range(heads):
            gain_ref[h * size : (h + 1) * size] = side[slim + h]
        total = jnp.zeros((chunk, size), F32)
        for i in range(near):
            grad = dot(rows_ref[i, tokens:], later_ref[i], 1, 1) * slope_ref[i].astype(F32)
            total = total + dot(grad.astype(BF), rows_ref[i, :tokens], 0, 0)
            total = total + parts_ref[i].astype(F32)[2 * chunk : 3 * chunk]
        pad = jnp.zeros((8, size), F32)
        total = jnp.concatenate([total, side[:slim], pad], axis=0).astype(BF)
        for i in range(far):
            out_ref[i] = total

    payload, later, grad_gain = run(
        later_kernel,
        [((far, chunk + slim + 8, size), BF), ((near, chunk, size), BF), ((width,), F32)],
        [parts, parts_far, group_rows, chunk_slope],
    )
    parts_far = swap(payload, "far")

    def weight_kernel(far_ref, later_ref, out_ref):
        total = far_ref[0].astype(F32)[:chunk]
        for i in range(1, far):
            total = total + far_ref[i].astype(F32)[:chunk]
        queries = [far_ref[i].astype(F32)[chunk : chunk + slim] for i in range(far)]
        total = jnp.concatenate([total] + queries, axis=0).astype(BF)
        for i in range(near):
            out_ref[i, :chunk] = later_ref[i]
            out_ref[i, chunk:] = total

    (payload,) = run(weight_kernel, [((near, 3 * chunk, size), BF)], [parts_far, later])
    done = swap(payload, "near")

    def last_kernel(
        in_ref, kg_ref, ks_ref, v_ref, wk_ref, gv_ref, kf_ref, gk_ref, gvalue_ref, gfq_ref, gfk_ref
    ):
        for h, at in enumerate(cols):
            mine = range(h * per_head, (h + 1) * per_head)
            later = jnp.concatenate([in_ref[j, :chunk] for j in mine], axis=0)
            grad = kg_ref[:, at].astype(F32) + dot(v_ref[:, at], later, 1, 1)
            grad = (grad * ks_ref[:, at].astype(F32)).astype(BF)
            gk_ref[:, at] = dot(grad, wk_ref[h], 1, 1).astype(BF)
            value = gv_ref[:, at].astype(F32) + dot(kf_ref[:, at], later, 1, 0)
            gvalue_ref[:, at] = value.astype(BF)
            rows = [in_ref[j, chunk : 2 * chunk].astype(F32) for j in mine]
            gfk_ref[h] = jnp.transpose(jnp.concatenate(rows, axis=0))
            rows = [in_ref[j, 2 * chunk :].astype(F32) for j in mine]
            gfq_ref[h] = jnp.concatenate(rows, axis=0)

    grad_key, grad_value, grad_feat_query, grad_feat_key = run(
        last_kernel,
        [((tokens, width), BF), ((tokens, width), BF), (feat_query.shape, F32), (feat_key.shape, F32)],
        [done, key_grad_local, key_slope, value_rows, feat_key, grad_value_local, key_feat],
    )
    return (attended, grad_query, grad_key, grad_value, grad_feat_query, grad_feat_key, grad_gain)


def solution(mesh):
    seq, head = mesh.devices.shape
    split = Mesh(mesh.devices.reshape(seq // NEAR, NEAR, head), ("far", "near", "head"))
    wide = P(("far", "near"), "head")
    per_head = P("head", None, None)
    in_specs = (wide, wide, wide, per_head, per_head, P("head"), wide)
    out_specs = (wide, wide, wide, wide, per_head, per_head, P("head"))
    return jax.shard_map(shards, mesh=split, in_specs=in_specs, out_specs=out_specs, check_vma=False)
```

```python
import jax
import jax.numpy as jnp
from jax import lax
from jax.experimental import pallas as pl
from jax.experimental.pallas import tpu as pltpu
from jax.sharding import Mesh, PartitionSpec as P

EPSILON = 1e-05
BF = jnp.bfloat16
F32 = jnp.float32
NEAR = 8
GAIN_ROWS = 16
STAT_ROWS = 8
TOKEN = ((8, 128), F32)
VMEM_BYTES = 24 * 1024 * 1024
WHOLE_VMEM = 64 * 1024 * 1024
STATE_VMEM = 63 * 1024 * 1024


def swap(x, axis):
    return lax.all_to_all(x, axis, 0, 0)


def run(kernel, outs, ins, after=(), fetch=(), limit=VMEM_BYTES):
    count, copies = len(ins), len(fetch)

    def body(*refs):
        sources = refs[count : count + copies]
        outputs = refs[count + copies + len(after) : count + copies + len(after) + len(outs)]
        if not copies:
            return kernel(*refs[:count], *outputs)
        held, sems = refs[-copies - 1 : -1], refs[-1]
        moves = [pltpu.make_async_copy(sources[i], held[i], sems.at[i]) for i in range(copies)]
        for move in moves:
            move.start()
        return kernel(*refs[:count], *held, *outputs, [move.wait for move in moves])

    whole = pl.BlockSpec(memory_space=pltpu.VMEM)
    far_off = pl.BlockSpec(memory_space=pl.ANY)
    scratch = [pltpu.VMEM(x.shape, x.dtype) for x in fetch]
    return pl.pallas_call(
        body,
        out_shape=[jax.ShapeDtypeStruct(shape, dtype) for shape, dtype in outs],
        in_specs=[whole] * count
        + [far_off] * copies
        + [far_off] * len(after),
        out_specs=[whole] * len(outs),
        scratch_shapes=scratch + [pltpu.SemaphoreType.DMA((copies,))] if copies else [],
        compiler_params=pltpu.CompilerParams(vmem_limit_bytes=limit),
        cost_estimate=pl.CostEstimate(flops=10**8, bytes_accessed=10**6, transcendentals=0),
    )(*ins, *fetch, *after)


def dot(a, b, over_a, over_b):
    return lax.dot_general(a, b, (((over_a,), (over_b,)), ((), ())), preferred_element_type=F32)


def silu_slope(x):
    g = 1.0 / (1.0 + jnp.exp(-x))
    return g * (1.0 + x * (1.0 - g))


def causal_mask(count, later=0):
    rows = lax.broadcasted_iota(jnp.int32, (count, count), later)
    cols = lax.broadcasted_iota(jnp.int32, (count, count), 1 - later)
    return rows >= cols


def shards(query_rows, key_rows, value_rows, feat_query, feat_key, norm_gain, grad_out):
    tokens, width = query_rows.shape
    heads, size = feat_query.shape[0], feat_query.shape[1]
    near, far = lax.axis_size("near"), lax.axis_size("far")
    full_width = width * lax.axis_size("head")
    chunk = heads * size // near
    slim = chunk // far
    per_head = near // heads
    gain_row = norm_gain.reshape(1, width)
    cols = [slice(h * size, (h + 1) * size) for h in range(heads)]

    def put_state(out_ref, h, value, row):
        for part in range(per_head):
            rows = value[part * chunk : (part + 1) * chunk]
            out_ref[h * per_head + part, row : row + chunk, :] = rows.astype(BF)

    def get_state(ref, h):
        parts = [ref[h * per_head + part] for part in range(per_head)]
        return jnp.concatenate(parts, axis=0)

    def pack_kernel(k_ref, v_ref, out_ref, held_ref, in_sems, out_sems):
        loads, stores = [], []
        for h, at in enumerate(cols):
            for i, ref in enumerate((k_ref, v_ref)):
                room = held_ref.at[h, pl.ds(i * tokens, tokens), :]
                loads.append(pltpu.make_async_copy(ref.at[:, at], room, in_sems.at[2 * h + i]))
        for load in loads:
            load.start()
        for h in range(heads):
            loads[2 * h].wait()
            loads[2 * h + 1].wait()
            for part in range(per_head):
                place = h * per_head + part
                store = pltpu.make_async_copy(held_ref.at[h], out_ref.at[place], out_sems.at[place])
                store.start()
                stores.append(store)
        for store in stores:
            store.wait()

    whole = pl.BlockSpec(memory_space=pltpu.VMEM)
    anywhere = pl.BlockSpec(memory_space=pl.ANY)
    payload = pl.pallas_call(
        pack_kernel,
        out_shape=jax.ShapeDtypeStruct((near, 2 * tokens, size), BF),
        in_specs=[anywhere, anywhere],
        out_specs=anywhere,
        scratch_shapes=[
            pltpu.VMEM((heads, 2 * tokens, size), BF),
            pltpu.SemaphoreType.DMA((2 * heads,)),
            pltpu.SemaphoreType.DMA((near,)),
        ],
        compiler_params=pltpu.CompilerParams(vmem_limit_bytes=WHOLE_VMEM),
        cost_estimate=pl.CostEstimate(flops=10**6, bytes_accessed=10**6, transcendentals=0),
    )(key_rows, value_rows)
    group_rows = swap(payload, "near")

    def feature_kernel(k_ref, wk_ref, q_ref, wq_ref, kf_ref, qf_ref):
        for h, at in enumerate(cols):
            pre = dot(k_ref[:, at], wk_ref[h], 1, 0)
            kf_ref[:, at] = (pre / (1.0 + jnp.exp(-pre))).astype(BF)
            pre = dot(q_ref[:, at], wq_ref[h], 1, 0)
            qf_ref[:, at] = (pre / (1.0 + jnp.exp(-pre))).astype(BF)

    key_feat, query_feat = run(
        feature_kernel,
        [((tokens, width), BF), ((tokens, width), BF)],
        [key_rows, feat_key, query_rows, feat_query],
    )

    def chunk_weights(wk_ref):
        member = lax.axis_index("near")
        weights = jnp.transpose(wk_ref[member // per_head].astype(F32))
        part = member % per_head
        mine = weights[:chunk]
        for other in range(1, per_head):
            mine = jnp.where(part == other, weights[other * chunk : (other + 1) * chunk], mine)
        return mine.astype(BF)

    def state_kernel(
        rows_ref, wk_ref, token_ref, parts_ref, slope_ref, out_ref, held_ref, wk_held, sems
    ):
        loads = [pltpu.make_async_copy(wk_ref, wk_held, sems.at[near])]
        for i in range(near):
            loads.append(pltpu.make_async_copy(rows_ref.at[i], held_ref.at[i], sems.at[i]))
        for load in loads:
            load.start()
        loads[0].wait()
        weights = chunk_weights(wk_held)
        total = jnp.zeros((chunk, size), F32)
        for i in range(near):
            loads[i + 1].wait()
            pre = dot(weights, held_ref[i, :tokens], 1, 1)
            gate = 1.0 / (1.0 + jnp.exp(-pre))
            slope_ref[i] = (gate * (1.0 + pre * (1.0 - gate))).astype(BF)
            state = dot((pre * gate).astype(BF), held_ref[i, tokens:], 1, 0)
            parts_ref[i] = state.astype(BF)
            total = total + state
        total = total.astype(BF)
        for i in range(far):
            out_ref[i] = total

    parts, chunk_slope, payload = pl.pallas_call(
        state_kernel,
        out_shape=[
            jax.ShapeDtypeStruct((near, chunk, size), BF),
            jax.ShapeDtypeStruct((near, chunk, tokens), BF),
            jax.ShapeDtypeStruct((far, chunk, size), BF),
        ],
        in_specs=[anywhere, anywhere, anywhere],
        out_specs=[whole] * 3,
        scratch_shapes=[
            pltpu.VMEM((near, 2 * tokens, size), BF),
            pltpu.VMEM(feat_key.shape, BF),
            pltpu.SemaphoreType.DMA((near + 1,)),
        ],
        compiler_params=pltpu.CompilerParams(vmem_limit_bytes=STATE_VMEM),
        cost_estimate=pl.CostEstimate(flops=10**8, bytes_accessed=10**6, transcendentals=0),
    )(group_rows, feat_key, query_feat)
    parts_far = swap(payload, "far")

    def join(parts_ref, far_ref, out_ref, backward):
        place = lax.axis_index("far")
        state = jnp.zeros((chunk, size), F32)
        for i in range(far):
            keep = (i > place) if backward else (i < place)
            state = state + jnp.where(keep, far_ref[i][:chunk].astype(F32), 0.0)
        for i in range(near - 1, -1, -1) if backward else range(near):
            out_ref[i] = state.astype(BF)
            state = state + parts_ref[i][:chunk].astype(F32)

    def prior_kernel(parts_ref, far_ref, out_ref):
        join(parts_ref, far_ref, out_ref, False)

    (payload,) = run(prior_kernel, [((near, chunk, size), BF)], [parts, parts_far])
    prior = swap(payload, "near")

    def norm_kernel(qf_ref, kf_ref, v_ref, p_ref, go_ref, gain_ref, pre_ref, gain_out, out_ref, waits):
        mask = causal_mask(tokens)
        squares = jnp.zeros((tokens, size), F32)
        inner = jnp.zeros((tokens, size), F32)
        for h, at in enumerate(cols):
            scores = jnp.where(mask, dot(qf_ref[:, at], kf_ref[:, at], 1, 1), 0.0).astype(BF)
            pre = dot(scores, v_ref[:, at], 1, 0) + dot(qf_ref[:, at], get_state(p_ref, h), 1, 0)
            pre_ref[:, at] = pre
            squares = squares + pre * pre
            if h == 0:
                waits[0]()
            inner = inner + go_ref[:, at].astype(F32) * gain_ref[:, at] * pre
        gain_out[...] = gain_ref[...]
        squares = jnp.sum(squares, axis=1, keepdims=True)
        inner = jnp.sum(inner, axis=1, keepdims=True)
        lane = lax.broadcasted_iota(jnp.int32, (tokens, size), 1)
        both = jnp.where(lane == 0, squares, jnp.where(lane == 1, inner, 0.0))
        rows = jnp.transpose(both)[:STAT_ROWS]
        for i in range(out_ref.shape[0]):
            out_ref[i] = rows

    peers = lax.axis_size("head")
    pre_norm, gain_row, payload = run(
        norm_kernel,
        [((tokens, width), F32), ((1, width), F32), ((peers, STAT_ROWS, tokens), F32)],
        [query_feat, key_feat, value_rows, prior, grad_out],
        fetch=[gain_row],
    )
    stats = swap(payload, "head")

    def row_factors(st_ref):
        rows = st_ref[0]
        for i in range(1, peers):
            rows = rows + st_ref[i]
        rows = jnp.concatenate([rows, jnp.zeros((size - STAT_ROWS, tokens), F32)], axis=0)
        both = jnp.transpose(rows)
        inverse = 1.0 / jnp.sqrt(both[:, 0:1] / full_width + EPSILON)
        return inverse, both[:, 1:2] * inverse / full_width

    def delta_of(at, inverse, slope, pre_ref, go_ref, gain_ref):
        normed = pre_ref[:, at] * inverse
        wide = go_ref[:, at].astype(F32)
        return ((wide * gain_ref[:, at] - normed * slope) * inverse).astype(BF), wide, normed

    def query_side(h, at, delta, mask, v_ref, kf_ref, p_ref, q_ref, wq_ref):
        back = jnp.where(mask, dot(delta, v_ref[:, at], 1, 1), 0.0).astype(BF)
        grad = dot(back, kf_ref[:, at], 1, 0) + dot(delta, get_state(p_ref, h), 1, 1)
        return (grad * silu_slope(dot(q_ref[:, at], wq_ref[h], 1, 0))).astype(BF)

    def key_side(at, delta, mask, v_ref, qf_ref):
        back = jnp.where(mask, dot(v_ref[:, at], delta, 1, 1), 0.0).astype(BF)
        return dot(back, qf_ref[:, at], 1, 0)

    def delta_kernel(st_ref, pre_ref, go_ref, gain_ref, qf_ref, v_ref, kf_ref, p_ref, q_ref, wq_ref, k_ref, wk_ref, out_ref):
        inverse, slope = row_factors(st_ref)
        mask, turned = causal_mask(tokens), causal_mask(tokens, 1)
        gains = []
        for h, at in enumerate(cols):
            delta, wide, normed = delta_of(at, inverse, slope, pre_ref, go_ref, gain_ref)
            gains.append(jnp.sum(wide * normed, axis=0, keepdims=True))
            put_state(out_ref, h, dot(qf_ref[:, at], delta, 0, 0), 0)
            grad = query_side(h, at, delta, mask, v_ref, kf_ref, p_ref, q_ref, wq_ref)
            put_state(out_ref, h, dot(q_ref[:, at], grad, 0, 0), chunk)
            grad = key_side(at, delta, turned, v_ref, qf_ref) * silu_slope(dot(k_ref[:, at], wk_ref[h], 1, 0))
            put_state(out_ref, h, dot(grad.astype(BF), k_ref[:, at], 0, 0), 2 * chunk)
        rest = [jnp.zeros((GAIN_ROWS - heads, size), F32)]
        rows = jnp.concatenate(gains + rest, axis=0).astype(BF)
        for i in range(near):
            out_ref[i, 3 * chunk :, :] = rows

    (payload,) = run(
        delta_kernel,
        [((near, 3 * chunk + GAIN_ROWS, size), BF)],
        [
            stats, pre_norm, grad_out, gain_row, query_feat, value_rows, key_feat, prior,
            query_rows, feat_query, key_rows, feat_key,
        ],
    )
    parts = swap(payload, "near")

    def local_kernel(
        st_ref, pre_ref, go_ref, gain_ref, qf_ref, v_ref, kf_ref, p_ref, q_ref, wq_ref, k_ref, wk_ref,
        att_ref, gq_ref, kg_ref, ks_ref, gv_ref, token_ref,
    ):
        token_ref[...] = jnp.zeros(token_ref.shape, F32)
        inverse, slope = row_factors(st_ref)
        mask, turned = causal_mask(tokens), causal_mask(tokens, 1)
        for h, at in enumerate(cols):
            delta, _, normed = delta_of(at, inverse, slope, pre_ref, go_ref, gain_ref)
            att_ref[:, at] = (normed * gain_ref[:, at]).astype(BF)
            grad = query_side(h, at, delta, mask, v_ref, kf_ref, p_ref, q_ref, wq_ref)
            gq_ref[:, at] = dot(grad, wq_ref[h], 1, 1).astype(BF)
            kg_ref[:, at] = key_side(at, delta, turned, v_ref, qf_ref).astype(BF)
            ks_ref[:, at] = silu_slope(dot(k_ref[:, at], wk_ref[h], 1, 0)).astype(BF)
            scores = jnp.where(turned, dot(kf_ref[:, at], qf_ref[:, at], 1, 1), 0.0).astype(BF)
            gv_ref[:, at] = dot(scores, delta, 1, 0).astype(BF)

    attended, grad_query, key_grad_local, key_slope, grad_value_local, token = run(
        local_kernel,
        [((tokens, width), BF)] * 5 + [TOKEN],
        [
            stats, pre_norm, grad_out, gain_row, query_feat, value_rows, key_feat, prior,
            query_rows, feat_query, key_rows, feat_key,
        ],
    )

    def back_total_kernel(in_ref, out_ref):
        total = in_ref[0].astype(F32)
        for i in range(1, near):
            total = total + in_ref[i].astype(F32)
        head_rows, gains = total[:chunk], total[3 * chunk : 3 * chunk + 8]
        for i in range(far):
            part = total[chunk + i * slim : chunk + (i + 1) * slim]
            out_ref[i] = jnp.concatenate([head_rows, part, gains], axis=0).astype(BF)

    (payload,) = run(
        back_total_kernel, [((far, chunk + slim + 8, size), BF)], [parts], after=[token]
    )
    parts_far = swap(payload, "far")

    def later_kernel(parts_ref, far_ref, rows_ref, slope_ref, out_ref, later_ref, gain_ref):
        join(parts_ref, far_ref, later_ref, True)
        side = far_ref[0].astype(F32)[chunk:]
        for i in range(1, far):
            side = side + far_ref[i].astype(F32)[chunk:]
        for h in range(heads):
            gain_ref[h * size : (h + 1) * size] = side[slim + h]
        total = jnp.zeros((chunk, size), F32)
        for i in range(near):
            grad = dot(later_ref[i], rows_ref[i, tokens:], 1, 1) * slope_ref[i].astype(F32)
            total = total + dot(grad.astype(BF), rows_ref[i, :tokens], 1, 0)
            total = total + parts_ref[i].astype(F32)[2 * chunk : 3 * chunk]
        pad = jnp.zeros((8, size), F32)
        total = jnp.concatenate([total, side[:slim], pad], axis=0).astype(BF)
        for i in range(far):
            out_ref[i] = total

    payload, later, grad_gain = run(
        later_kernel,
        [((far, chunk + slim + 8, size), BF), ((near, chunk, size), BF), ((width,), F32)],
        [parts, parts_far, group_rows, chunk_slope],
    )
    parts_far = swap(payload, "far")

    def weight_kernel(far_ref, later_ref, out_ref):
        total = far_ref[0].astype(F32)[:chunk]
        for i in range(1, far):
            total = total + far_ref[i].astype(F32)[:chunk]
        queries = [far_ref[i].astype(F32)[chunk : chunk + slim] for i in range(far)]
        total = jnp.concatenate([total] + queries, axis=0).astype(BF)
        for i in range(near):
            out_ref[i, :chunk] = later_ref[i]
            out_ref[i, chunk:] = total

    (payload,) = run(weight_kernel, [((near, 3 * chunk, size), BF)], [parts_far, later])
    done = swap(payload, "near")

    def last_kernel(
        in_ref, kg_ref, ks_ref, v_ref, wk_ref, gv_ref, kf_ref, gk_ref, gvalue_ref, gfq_ref, gfk_ref
    ):
        for h, at in enumerate(cols):
            mine = range(h * per_head, (h + 1) * per_head)
            later = jnp.concatenate([in_ref[j, :chunk] for j in mine], axis=0)
            grad = kg_ref[:, at].astype(F32) + dot(v_ref[:, at], later, 1, 1)
            grad = (grad * ks_ref[:, at].astype(F32)).astype(BF)
            gk_ref[:, at] = dot(grad, wk_ref[h], 1, 1).astype(BF)
            value = gv_ref[:, at].astype(F32) + dot(kf_ref[:, at], later, 1, 0)
            gvalue_ref[:, at] = value.astype(BF)
            rows = [in_ref[j, chunk : 2 * chunk].astype(F32) for j in mine]
            gfk_ref[h] = jnp.transpose(jnp.concatenate(rows, axis=0))
            rows = [in_ref[j, 2 * chunk :].astype(F32) for j in mine]
            gfq_ref[h] = jnp.concatenate(rows, axis=0)

    grad_key, grad_value, grad_feat_query, grad_feat_key = run(
        last_kernel,
        [((tokens, width), BF), ((tokens, width), BF), (feat_query.shape, F32), (feat_key.shape, F32)],
        [done, key_grad_local, key_slope, value_rows, feat_key, grad_value_local, key_feat],
    )
    return (attended, grad_query, grad_key, grad_value, grad_feat_query, grad_feat_key, grad_gain)


def solution(mesh):
    seq, head = mesh.devices.shape
    split = Mesh(mesh.devices.reshape(seq // NEAR, NEAR, head), ("far", "near", "head"))
    wide = P(("far", "near"), "head")
    per_head = P("head", None, None)
    in_specs = (wide, wide, wide, per_head, per_head, P("head"), wide)
    out_specs = (wide, wide, wide, wide, per_head, per_head, P("head"))
    return jax.shard_map(shards, mesh=split, in_specs=in_specs, out_specs=out_specs, check_vma=False)
```

```python
import jax
import jax.numpy as jnp
from jax import lax
from jax.experimental import pallas as pl
from jax.experimental.pallas import tpu as pltpu
from jax.sharding import Mesh, PartitionSpec as P

EPSILON = 1e-05
BF = jnp.bfloat16
F32 = jnp.float32
NEAR = 8
GAIN_ROWS = 16
STAT_ROWS = 8
TOKEN = ((8, 128), F32)
VMEM_BYTES = 24 * 1024 * 1024
WHOLE_VMEM = 64 * 1024 * 1024


def swap(x, axis):
    return lax.all_to_all(x, axis, 0, 0)


def run(kernel, outs, ins, after=(), fetch=(), limit=VMEM_BYTES):
    count, copies = len(ins), len(fetch)

    def body(*refs):
        sources = refs[count : count + copies]
        outputs = refs[count + copies + len(after) : count + copies + len(after) + len(outs)]
        if not copies:
            return kernel(*refs[:count], *outputs)
        held, sems = refs[-copies - 1 : -1], refs[-1]
        moves = [pltpu.make_async_copy(sources[i], held[i], sems.at[i]) for i in range(copies)]
        for move in moves:
            move.start()
        return kernel(*refs[:count], *held, *outputs, [move.wait for move in moves])

    whole = pl.BlockSpec(memory_space=pltpu.VMEM)
    far_off = pl.BlockSpec(memory_space=pl.ANY)
    scratch = [pltpu.VMEM(x.shape, x.dtype) for x in fetch]
    return pl.pallas_call(
        body,
        out_shape=[jax.ShapeDtypeStruct(shape, dtype) for shape, dtype in outs],
        in_specs=[whole] * count
        + [far_off] * copies
        + [far_off] * len(after),
        out_specs=[whole] * len(outs),
        scratch_shapes=scratch + [pltpu.SemaphoreType.DMA((copies,))] if copies else [],
        compiler_params=pltpu.CompilerParams(vmem_limit_bytes=limit),
        cost_estimate=pl.CostEstimate(flops=10**8, bytes_accessed=10**6, transcendentals=0),
    )(*ins, *fetch, *after)


def dot(a, b, over_a, over_b):
    return lax.dot_general(a, b, (((over_a,), (over_b,)), ((), ())), preferred_element_type=F32)


def silu_slope(x):
    g = 1.0 / (1.0 + jnp.exp(-x))
    return g * (1.0 + x * (1.0 - g))


def causal_mask(count, later=0):
    rows = lax.broadcasted_iota(jnp.int32, (count, count), later)
    cols = lax.broadcasted_iota(jnp.int32, (count, count), 1 - later)
    return rows >= cols


def shards(query_rows, key_rows, value_rows, feat_query, feat_key, norm_gain, grad_out):
    tokens, width = query_rows.shape
    heads, size = feat_query.shape[0], feat_query.shape[1]
    near, far = lax.axis_size("near"), lax.axis_size("far")
    full_width = width * lax.axis_size("head")
    chunk = heads * size // near
    slim = chunk // far
    per_head = near // heads
    cols = [slice(h * size, (h + 1) * size) for h in range(heads)]

    def put_state(out_ref, h, value, row):
        for part in range(per_head):
            rows = value[part * chunk : (part + 1) * chunk]
            out_ref[h * per_head + part, row : row + chunk, :] = rows.astype(BF)

    def get_state(ref, h):
        parts = [ref[h * per_head + part] for part in range(per_head)]
        return jnp.concatenate(parts, axis=0)

    def state_kernel(wk_ref, k_ref, v_ref, wq_ref, q_ref, gain_ref, kf_ref, qf_ref, out_ref, row_ref, waits):
        waits[0]()
        waits[1]()
        for h, at in enumerate(cols):
            pre = dot(k_ref[:, at], wk_ref[h], 1, 0)
            kf_ref[:, at] = (pre / (1.0 + jnp.exp(-pre))).astype(BF)
        waits[2]()
        for h, at in enumerate(cols):
            put_state(out_ref, h, dot(kf_ref[:, at], v_ref[:, at], 0, 0), 0)
        for wait in waits[3:]:
            wait()
        for h, at in enumerate(cols):
            pre = dot(q_ref[:, at], wq_ref[h], 1, 0)
            qf_ref[:, at] = (pre / (1.0 + jnp.exp(-pre))).astype(BF)
            row_ref[:, at] = jnp.broadcast_to(gain_ref[at].reshape(1, size), (8, size))

    key_feat, query_feat, payload, gain_rows = run(
        state_kernel,
        [((tokens, width), BF), ((tokens, width), BF), ((near, chunk, size), BF), ((8, width), F32)],
        [],
        fetch=[feat_key, key_rows, value_rows, feat_query, query_rows, norm_gain],
        limit=WHOLE_VMEM,
    )
    parts = swap(payload, "near")

    def total_kernel(in_ref, out_ref):
        total = in_ref[0].astype(F32)
        for i in range(1, near):
            total = total + in_ref[i].astype(F32)
        total = total.astype(BF)
        for i in range(out_ref.shape[0]):
            out_ref[i] = total

    (payload,) = run(total_kernel, [((far, chunk, size), BF)], [parts])
    parts_far = swap(payload, "far")

    def join(parts_ref, far_ref, out_ref, backward):
        place = lax.axis_index("far")
        state = jnp.zeros((chunk, size), F32)
        for i in range(far):
            keep = (i > place) if backward else (i < place)
            state = state + jnp.where(keep, far_ref[i][:chunk].astype(F32), 0.0)
        for i in range(near - 1, -1, -1) if backward else range(near):
            out_ref[i] = state.astype(BF)
            state = state + parts_ref[i][:chunk].astype(F32)

    def prior_kernel(parts_ref, far_ref, out_ref):
        join(parts_ref, far_ref, out_ref, False)

    (payload,) = run(prior_kernel, [((near, chunk, size), BF)], [parts, parts_far])
    prior = swap(payload, "near")

    def norm_kernel(qf_ref, kf_ref, v_ref, p_ref, go_ref, gain_ref, pre_ref, out_ref):
        mask = causal_mask(tokens)
        squares = jnp.zeros((tokens, size), F32)
        inner = jnp.zeros((tokens, size), F32)
        for h, at in enumerate(cols):
            scores = jnp.where(mask, dot(qf_ref[:, at], kf_ref[:, at], 1, 1), 0.0).astype(BF)
            pre = dot(scores, v_ref[:, at], 1, 0) + dot(qf_ref[:, at], get_state(p_ref, h), 1, 0)
            pre_ref[:, at] = pre
            squares = squares + pre * pre
            inner = inner + go_ref[:, at].astype(F32) * gain_ref[:1, at] * pre
        squares = jnp.sum(squares, axis=1, keepdims=True)
        inner = jnp.sum(inner, axis=1, keepdims=True)
        lane = lax.broadcasted_iota(jnp.int32, (tokens, size), 1)
        both = jnp.where(lane == 0, squares, jnp.where(lane == 1, inner, 0.0))
        rows = jnp.transpose(both)[:STAT_ROWS]
        for i in range(out_ref.shape[0]):
            out_ref[i] = rows

    peers = lax.axis_size("head")
    pre_norm, payload = run(
        norm_kernel,
        [((tokens, width), F32), ((peers, STAT_ROWS, tokens), F32)],
        [query_feat, key_feat, value_rows, prior, grad_out, gain_rows],
    )
    stats = swap(payload, "head")

    def row_factors(st_ref):
        rows = st_ref[0]
        for i in range(1, peers):
            rows = rows + st_ref[i]
        rows = jnp.concatenate([rows, jnp.zeros((size - STAT_ROWS, tokens), F32)], axis=0)
        both = jnp.transpose(rows)
        inverse = 1.0 / jnp.sqrt(both[:, 0:1] / full_width + EPSILON)
        return inverse, both[:, 1:2] * inverse / full_width

    def query_side(h, at, delta, mask, v_ref, kf_ref, p_ref, q_ref, wq_ref):
        back = jnp.where(mask, dot(delta, v_ref[:, at], 1, 1), 0.0).astype(BF)
        grad = dot(back, kf_ref[:, at], 1, 0) + dot(delta, get_state(p_ref, h), 1, 1)
        return (grad * silu_slope(dot(q_ref[:, at], wq_ref[h], 1, 0))).astype(BF)

    def delta_kernel(
        st_ref, pre_ref, go_ref, gain_ref, qf_ref, v_ref, kf_ref, p_ref, q_ref, wq_ref, att_ref, delta_ref, out_ref
    ):
        inverse, slope = row_factors(st_ref)
        mask = causal_mask(tokens)
        gains = []
        for h, at in enumerate(cols):
            normed = pre_ref[:, at] * inverse
            wide = go_ref[:, at].astype(F32)
            delta = ((wide * gain_ref[:1, at] - normed * slope) * inverse).astype(BF)
            delta_ref[:, at] = delta
            att_ref[:, at] = (normed * gain_ref[:1, at]).astype(BF)
            gains.append(jnp.sum(wide * normed, axis=0, keepdims=True))
            put_state(out_ref, h, dot(qf_ref[:, at], delta, 0, 0), 0)
            grad = query_side(h, at, delta, mask, v_ref, kf_ref, p_ref, q_ref, wq_ref)
            put_state(out_ref, h, dot(q_ref[:, at], grad, 0, 0), chunk)
        rest = [jnp.zeros((GAIN_ROWS - heads, size), F32)]
        rows = jnp.concatenate(gains + rest, axis=0).astype(BF)
        for i in range(near):
            out_ref[i, 2 * chunk :, :] = rows

    attended, delta, payload = run(
        delta_kernel,
        [((tokens, width), BF), ((tokens, width), BF), ((near, 2 * chunk + GAIN_ROWS, size), BF)],
        [stats, pre_norm, grad_out, gain_rows, query_feat, value_rows, key_feat, prior, query_rows, feat_query],
    )
    parts = swap(payload, "near")

    def back_total_kernel(in_ref, out_ref):
        total = in_ref[0].astype(F32)
        for i in range(1, near):
            total = total + in_ref[i].astype(F32)
        head_rows, gains = total[:chunk], total[2 * chunk : 2 * chunk + 8]
        for i in range(far):
            part = total[chunk + i * slim : chunk + (i + 1) * slim]
            out_ref[i] = jnp.concatenate([head_rows, part, gains], axis=0).astype(BF)

    (payload,) = run(
        back_total_kernel, [((far, chunk + slim + 8, size), BF)], [parts]
    )
    parts_far = swap(payload, "far")

    def later_kernel(parts_ref, far_ref, out_ref, side_ref, gain_ref):
        join(parts_ref, far_ref, out_ref, True)
        side = far_ref[0].astype(F32)[chunk:]
        for i in range(1, far):
            side = side + far_ref[i].astype(F32)[chunk:]
        side_ref[...] = side
        for h, at in enumerate(cols):
            gain_ref[at] = side[slim + h]

    payload, side, grad_gain = run(
        later_kernel,
        [((near, chunk, size), BF), ((slim + 8, size), F32), ((width,), F32)],
        [parts, parts_far],
    )
    later = swap(payload, "near")

    def key_kernel(delta_ref, qf_ref, v_ref, l_ref, wk_ref, k_ref, kpg_ref, out_ref):
        turned = causal_mask(tokens, 1)
        for h, at in enumerate(cols):
            back = jnp.where(turned, dot(v_ref[:, at], delta_ref[:, at], 1, 1), 0.0).astype(BF)
            grad = dot(back, qf_ref[:, at], 1, 0) + dot(v_ref[:, at], get_state(l_ref, h), 1, 1)
            grad = (grad * silu_slope(dot(k_ref[:, at], wk_ref[h], 1, 0))).astype(BF)
            kpg_ref[:, at] = grad
            put_state(out_ref, h, dot(k_ref[:, at], grad, 0, 0), 0)

    key_pre_grad, payload = run(
        key_kernel,
        [((tokens, width), BF), ((near, chunk, size), BF)],
        [delta, query_feat, value_rows, later, feat_key, key_rows],
    )
    parts = swap(payload, "near")

    def last_kernel(
        kpg_ref, wk_ref, l_ref, delta_ref, qf_ref, kf_ref, v_ref, p_ref, q_ref, wq_ref,
        gk_ref, gq_ref, gv_ref, token_ref,
    ):
        token_ref[...] = jnp.zeros(token_ref.shape, F32)
        mask, turned = causal_mask(tokens), causal_mask(tokens, 1)
        for h, at in enumerate(cols):
            gk_ref[:, at] = dot(kpg_ref[:, at], wk_ref[h], 1, 1).astype(BF)
            delta = delta_ref[:, at]
            grad = query_side(h, at, delta, mask, v_ref, kf_ref, p_ref, q_ref, wq_ref)
            gq_ref[:, at] = dot(grad, wq_ref[h], 1, 1).astype(BF)
            scores = jnp.where(turned, dot(kf_ref[:, at], qf_ref[:, at], 1, 1), 0.0).astype(BF)
            value = dot(scores, delta, 1, 0) + dot(kf_ref[:, at], get_state(l_ref, h), 1, 0)
            gv_ref[:, at] = value.astype(BF)

    grad_key, grad_query, grad_value, token = run(
        last_kernel,
        [((tokens, width), BF)] * 3 + [TOKEN],
        [
            key_pre_grad, feat_key, later, delta, query_feat, key_feat, value_rows, prior, query_rows, feat_query,
        ],
    )

    def weight_total_kernel(in_ref, side_ref, out_ref):
        total = in_ref[0].astype(F32)
        for i in range(1, near):
            total = total + in_ref[i].astype(F32)
        pad = jnp.zeros((8, size), F32)
        total = jnp.concatenate([total, side_ref[:slim], pad], axis=0).astype(BF)
        for i in range(far):
            out_ref[i] = total

    (payload,) = run(
        weight_total_kernel,
        [((far, chunk + slim + 8, size), BF)],
        [parts, side],
        after=[token],
    )
    parts_far = swap(payload, "far")

    def weight_kernel(far_ref, out_ref):
        total = far_ref[0].astype(F32)[:chunk]
        for i in range(1, far):
            total = total + far_ref[i].astype(F32)[:chunk]
        queries = [far_ref[i].astype(F32)[chunk : chunk + slim] for i in range(far)]
        total = jnp.concatenate([total] + queries, axis=0).astype(BF)
        for i in range(near):
            out_ref[i] = total

    (payload,) = run(weight_kernel, [((near, 2 * chunk, size), BF)], [parts_far])
    done = swap(payload, "near")

    def widen_kernel(in_ref, gq_ref, gk_ref):
        for h in range(heads):
            for part in range(per_head):
                rows = slice(part * chunk, (part + 1) * chunk)
                gk_ref[h, rows] = in_ref[h * per_head + part, :chunk].astype(F32)
                gq_ref[h, rows] = in_ref[h * per_head + part, chunk:].astype(F32)

    grad_feat_query, grad_feat_key = run(
        widen_kernel, [(feat_query.shape, F32), (feat_key.shape, F32)], [done]
    )
    return (attended, grad_query, grad_key, grad_value, grad_feat_query, grad_feat_key, grad_gain)


def solution(mesh):
    seq, head = mesh.devices.shape
    split = Mesh(mesh.devices.reshape(seq // NEAR, NEAR, head), ("far", "near", "head"))
    wide = P(("far", "near"), "head")
    per_head = P("head", None, None)
    in_specs = (wide, wide, wide, per_head, per_head, P("head"), wide)
    out_specs = (wide, wide, wide, wide, per_head, per_head, P("head"))
    return jax.shard_map(shards, mesh=split, in_specs=in_specs, out_specs=out_specs, check_vma=False)
```

```python
import jax
import jax.numpy as jnp
from jax import lax
from jax.experimental import pallas as pl
from jax.experimental.pallas import tpu as pltpu
from jax.sharding import Mesh, PartitionSpec as P

EPSILON = 1e-05
BF = jnp.bfloat16
F32 = jnp.float32
NEAR = 8
GAIN_ROWS = 16
STAT_ROWS = 8
TOKEN = ((8, 128), F32)
VMEM_BYTES = 24 * 1024 * 1024
WHOLE_VMEM = 64 * 1024 * 1024


def swap(x, axis):
    return lax.all_to_all(x, axis, 0, 0)


def run(kernel, outs, ins, after=()):
    count = len(ins)

    def body(*refs):
        kernel(*refs[:count], *refs[count + len(after) :])

    whole = pl.BlockSpec(memory_space=pltpu.VMEM)
    return pl.pallas_call(
        body,
        out_shape=[jax.ShapeDtypeStruct(shape, dtype) for shape, dtype in outs],
        in_specs=[whole] * count + [pl.BlockSpec(memory_space=pl.ANY)] * len(after),
        out_specs=[whole] * len(outs),
        compiler_params=pltpu.CompilerParams(vmem_limit_bytes=VMEM_BYTES),
        cost_estimate=pl.CostEstimate(flops=10**8, bytes_accessed=10**6, transcendentals=0),
    )(*ins, *after)


def dot(a, b, over_a, over_b):
    return lax.dot_general(a, b, (((over_a,), (over_b,)), ((), ())), preferred_element_type=F32)


def silu_slope(x):
    g = 1.0 / (1.0 + jnp.exp(-x))
    return g * (1.0 + x * (1.0 - g))


def causal_mask(count, later=0):
    rows = lax.broadcasted_iota(jnp.int32, (count, count), later)
    cols = lax.broadcasted_iota(jnp.int32, (count, count), 1 - later)
    return rows >= cols


def shards(query_rows, key_rows, value_rows, feat_query, feat_key, norm_gain, grad_out):
    tokens, width = query_rows.shape
    heads, size = feat_query.shape[0], feat_query.shape[1]
    near, far = lax.axis_size("near"), lax.axis_size("far")
    full_width = width * lax.axis_size("head")
    chunk = heads * size // near
    slim = chunk // far
    per_head = near // heads
    cols = [slice(h * size, (h + 1) * size) for h in range(heads)]

    def put_state(out_ref, h, value, row):
        for part in range(per_head):
            rows = value[part * chunk : (part + 1) * chunk]
            out_ref[h * per_head + part, row : row + chunk, :] = rows.astype(BF)

    def get_state(ref, h):
        parts = [ref[h * per_head + part] for part in range(per_head)]
        return jnp.concatenate(parts, axis=0)

    quarter = tokens // 4
    blocks = [pl.ds(i * quarter, quarter) for i in range(4)]

    def state_kernel(
        wk_hbm, k_hbm, v_hbm, wq_hbm, q_hbm, gain_hbm, kf_hbm, qf_hbm, out_hbm, row_hbm,
        wk_ref, k_ref, v_ref, wq_ref, q_ref, gain_ref, kf_ref, qf_ref, out_ref, row_ref, in_sems, out_sems,
    ):
        loads, stores = [], []

        def load(source, target):
            move = pltpu.make_async_copy(source, target, in_sems.at[len(loads)])
            move.start()
            loads.append(move)

        def store(source, target):
            move = pltpu.make_async_copy(source, target, out_sems.at[len(stores)])
            move.start()
            stores.append(move)

        def load_rows(source, target):
            for rows in blocks:
                load(source.at[rows, :], target.at[rows, :])

        load(wk_hbm, wk_ref)
        load_rows(k_hbm, k_ref)
        load_rows(v_hbm, v_ref)
        load(wq_hbm, wq_ref)
        load_rows(q_hbm, q_ref)
        load(gain_hbm, gain_ref)
        for move in loads[:5]:
            move.wait()
        for h, at in enumerate(cols):
            pre = dot(k_ref[:, at], wk_ref[h], 1, 0)
            kf_ref[:, at] = (pre / (1.0 + jnp.exp(-pre))).astype(BF)
            store(kf_ref.at[:, at], kf_hbm.at[:, at])
        for move in loads[5:9]:
            move.wait()
        for h, at in enumerate(cols):
            put_state(out_ref, h, dot(kf_ref[:, at], v_ref[:, at], 0, 0), 0)
            own = pl.ds(h * per_head, per_head)
            store(out_ref.at[own], out_hbm.at[own])
        for move in loads[9:]:
            move.wait()
        for h, at in enumerate(cols):
            row_ref[:, at] = jnp.broadcast_to(gain_ref[at].reshape(1, size), (8, size))
        store(row_ref, row_hbm)
        for h, at in enumerate(cols):
            pre = dot(q_ref[:, at], wq_ref[h], 1, 0)
            qf_ref[:, at] = (pre / (1.0 + jnp.exp(-pre))).astype(BF)
            store(qf_ref.at[:, at], qf_hbm.at[:, at])
        for move in stores:
            move.wait()

    anywhere = pl.BlockSpec(memory_space=pl.ANY)
    inputs = [feat_key, key_rows, value_rows, feat_query, query_rows, norm_gain]
    results = [
        jax.ShapeDtypeStruct((tokens, width), BF),
        jax.ShapeDtypeStruct((tokens, width), BF),
        jax.ShapeDtypeStruct((near, chunk, size), BF),
        jax.ShapeDtypeStruct((8, width), F32),
    ]
    key_feat, query_feat, payload, gain_rows = pl.pallas_call(
        state_kernel,
        out_shape=results,
        in_specs=[anywhere] * len(inputs),
        out_specs=[anywhere] * len(results),
        scratch_shapes=[pltpu.VMEM(x.shape, x.dtype) for x in inputs + results]
        + [pltpu.SemaphoreType.DMA((15,)), pltpu.SemaphoreType.DMA((3 * heads + 1,))],
        compiler_params=pltpu.CompilerParams(vmem_limit_bytes=WHOLE_VMEM),
        cost_estimate=pl.CostEstimate(flops=10**8, bytes_accessed=10**6, transcendentals=0),
    )(*inputs)
    parts = swap(payload, "near")

    def total_kernel(in_ref, out_ref):
        total = in_ref[0].astype(F32)
        for i in range(1, near):
            total = total + in_ref[i].astype(F32)
        total = total.astype(BF)
        for i in range(out_ref.shape[0]):
            out_ref[i] = total

    (payload,) = run(total_kernel, [((far, chunk, size), BF)], [parts])
    parts_far = swap(payload, "far")

    def join(parts_ref, far_ref, out_ref, backward):
        place = lax.axis_index("far")
        state = jnp.zeros((chunk, size), F32)
        for i in range(far):
            keep = (i > place) if backward else (i < place)
            state = state + jnp.where(keep, far_ref[i][:chunk].astype(F32), 0.0)
        for i in range(near - 1, -1, -1) if backward else range(near):
            out_ref[i] = state.astype(BF)
            state = state + parts_ref[i][:chunk].astype(F32)

    def prior_kernel(parts_ref, far_ref, out_ref):
        join(parts_ref, far_ref, out_ref, False)

    (payload,) = run(prior_kernel, [((near, chunk, size), BF)], [parts, parts_far])
    prior = swap(payload, "near")

    def norm_kernel(qf_ref, kf_ref, v_ref, p_ref, go_ref, gain_ref, pre_ref, out_ref):
        mask = causal_mask(tokens)
        squares = jnp.zeros((tokens, size), F32)
        inner = jnp.zeros((tokens, size), F32)
        for h, at in enumerate(cols):
            scores = jnp.where(mask, dot(qf_ref[:, at], kf_ref[:, at], 1, 1), 0.0).astype(BF)
            pre = dot(scores, v_ref[:, at], 1, 0) + dot(qf_ref[:, at], get_state(p_ref, h), 1, 0)
            pre_ref[:, at] = pre
            squares = squares + pre * pre
            inner = inner + go_ref[:, at].astype(F32) * gain_ref[:1, at] * pre
        squares = jnp.sum(squares, axis=1, keepdims=True)
        inner = jnp.sum(inner, axis=1, keepdims=True)
        lane = lax.broadcasted_iota(jnp.int32, (tokens, size), 1)
        both = jnp.where(lane == 0, squares, jnp.where(lane == 1, inner, 0.0))
        rows = jnp.transpose(both)[:STAT_ROWS]
        for i in range(out_ref.shape[0]):
            out_ref[i] = rows

    peers = lax.axis_size("head")
    pre_norm, payload = run(
        norm_kernel,
        [((tokens, width), F32), ((peers, STAT_ROWS, tokens), F32)],
        [query_feat, key_feat, value_rows, prior, grad_out, gain_rows],
    )
    stats = swap(payload, "head")

    def row_factors(st_ref):
        rows = st_ref[0]
        for i in range(1, peers):
            rows = rows + st_ref[i]
        rows = jnp.concatenate([rows, jnp.zeros((size - STAT_ROWS, tokens), F32)], axis=0)
        both = jnp.transpose(rows)
        inverse = 1.0 / jnp.sqrt(both[:, 0:1] / full_width + EPSILON)
        return inverse, both[:, 1:2] * inverse / full_width

    def query_side(h, at, delta, mask, v_ref, kf_ref, p_ref, q_ref, wq_ref):
        back = jnp.where(mask, dot(delta, v_ref[:, at], 1, 1), 0.0).astype(BF)
        grad = dot(back, kf_ref[:, at], 1, 0) + dot(delta, get_state(p_ref, h), 1, 1)
        return (grad * silu_slope(dot(q_ref[:, at], wq_ref[h], 1, 0))).astype(BF)

    def delta_kernel(
        st_ref, pre_ref, go_ref, gain_ref, qf_ref, v_ref, kf_ref, p_ref, q_ref, wq_ref, att_ref, delta_ref, out_ref
    ):
        inverse, slope = row_factors(st_ref)
        mask = causal_mask(tokens)
        gains = []
        for h, at in enumerate(cols):
            normed = pre_ref[:, at] * inverse
            wide = go_ref[:, at].astype(F32)
            delta = ((wide * gain_ref[:1, at] - normed * slope) * inverse).astype(BF)
            delta_ref[:, at] = delta
            att_ref[:, at] = (normed * gain_ref[:1, at]).astype(BF)
            gains.append(jnp.sum(wide * normed, axis=0, keepdims=True))
            put_state(out_ref, h, dot(qf_ref[:, at], delta, 0, 0), 0)
            grad = query_side(h, at, delta, mask, v_ref, kf_ref, p_ref, q_ref, wq_ref)
            put_state(out_ref, h, dot(q_ref[:, at], grad, 0, 0), chunk)
        rest = [jnp.zeros((GAIN_ROWS - heads, size), F32)]
        rows = jnp.concatenate(gains + rest, axis=0).astype(BF)
        for i in range(near):
            out_ref[i, 2 * chunk :, :] = rows

    attended_near, delta, payload = run(
        delta_kernel,
        [((tokens, width), BF), ((tokens, width), BF), ((near, 2 * chunk + GAIN_ROWS, size), BF)],
        [stats, pre_norm, grad_out, gain_rows, query_feat, value_rows, key_feat, prior, query_rows, feat_query],
    )
    parts = swap(payload, "near")

    def back_total_kernel(in_ref, out_ref):
        total = in_ref[0].astype(F32)
        for i in range(1, near):
            total = total + in_ref[i].astype(F32)
        head_rows, gains = total[:chunk], total[2 * chunk : 2 * chunk + 8]
        for i in range(far):
            part = total[chunk + i * slim : chunk + (i + 1) * slim]
            out_ref[i] = jnp.concatenate([head_rows, part, gains], axis=0).astype(BF)

    (payload,) = run(
        back_total_kernel, [((far, chunk + slim + 8, size), BF)], [parts]
    )
    parts_far = swap(payload, "far")

    def later_kernel(parts_ref, far_ref, out_ref, side_ref):
        join(parts_ref, far_ref, out_ref, True)
        side = far_ref[0].astype(F32)[chunk:]
        for i in range(1, far):
            side = side + far_ref[i].astype(F32)[chunk:]
        side_ref[...] = side

    payload, side = run(
        later_kernel,
        [((near, chunk, size), BF), ((slim + 8, size), F32)],
        [parts, parts_far],
    )
    later = swap(payload, "near")

    def key_kernel(delta_ref, qf_ref, v_ref, l_ref, wk_ref, k_ref, kpg_ref, out_ref):
        turned = causal_mask(tokens, 1)
        for h, at in enumerate(cols):
            back = jnp.where(turned, dot(v_ref[:, at], delta_ref[:, at], 1, 1), 0.0).astype(BF)
            grad = dot(back, qf_ref[:, at], 1, 0) + dot(v_ref[:, at], get_state(l_ref, h), 1, 1)
            grad = (grad * silu_slope(dot(k_ref[:, at], wk_ref[h], 1, 0))).astype(BF)
            kpg_ref[:, at] = grad
            put_state(out_ref, h, dot(k_ref[:, at], grad, 0, 0), 0)

    key_pre_grad, payload = run(
        key_kernel,
        [((tokens, width), BF), ((near, chunk, size), BF)],
        [delta, query_feat, value_rows, later, feat_key, key_rows],
    )
    parts = swap(payload, "near")

    def last_kernel(
        kpg_ref, wk_ref, l_ref, delta_ref, qf_ref, kf_ref, v_ref, p_ref, q_ref, wq_ref, att_ref, side_ref,
        gk_ref, gq_ref, gv_ref, out_ref, gain_ref, token_ref,
    ):
        out_ref[...] = att_ref[...]
        for h, at in enumerate(cols):
            gain_ref[at] = side_ref[slim + h]
        token_ref[...] = jnp.zeros(token_ref.shape, F32)
        mask, turned = causal_mask(tokens), causal_mask(tokens, 1)
        for h, at in enumerate(cols):
            gk_ref[:, at] = dot(kpg_ref[:, at], wk_ref[h], 1, 1).astype(BF)
            delta = delta_ref[:, at]
            grad = query_side(h, at, delta, mask, v_ref, kf_ref, p_ref, q_ref, wq_ref)
            gq_ref[:, at] = dot(grad, wq_ref[h], 1, 1).astype(BF)
            scores = jnp.where(turned, dot(kf_ref[:, at], qf_ref[:, at], 1, 1), 0.0).astype(BF)
            value = dot(scores, delta, 1, 0) + dot(kf_ref[:, at], get_state(l_ref, h), 1, 0)
            gv_ref[:, at] = value.astype(BF)

    grad_key, grad_query, grad_value, attended, grad_gain, token = run(
        last_kernel,
        [((tokens, width), BF)] * 4 + [((width,), F32), TOKEN],
        [
            key_pre_grad, feat_key, later, delta, query_feat, key_feat, value_rows, prior, query_rows, feat_query,
            attended_near, side,
        ],
    )

    def weight_total_kernel(in_ref, side_ref, out_ref):
        total = in_ref[0].astype(F32)
        for i in range(1, near):
            total = total + in_ref[i].astype(F32)
        pad = jnp.zeros((8, size), F32)
        total = jnp.concatenate([total, side_ref[:slim], pad], axis=0).astype(BF)
        for i in range(far):
            out_ref[i] = total

    (payload,) = run(
        weight_total_kernel,
        [((far, chunk + slim + 8, size), BF)],
        [parts, side],
        after=[token],
    )
    parts_far = swap(payload, "far")

    def weight_kernel(far_ref, out_ref):
        total = far_ref[0].astype(F32)[:chunk]
        for i in range(1, far):
            total = total + far_ref[i].astype(F32)[:chunk]
        queries = [far_ref[i].astype(F32)[chunk : chunk + slim] for i in range(far)]
        total = jnp.concatenate([total] + queries, axis=0).astype(BF)
        for i in range(near):
            out_ref[i] = total

    (payload,) = run(weight_kernel, [((near, 2 * chunk, size), BF)], [parts_far])
    done = swap(payload, "near")

    def widen_kernel(in_ref, gq_ref, gk_ref):
        for h in range(heads):
            for part in range(per_head):
                rows = slice(part * chunk, (part + 1) * chunk)
                gk_ref[h, rows] = in_ref[h * per_head + part, :chunk].astype(F32)
                gq_ref[h, rows] = in_ref[h * per_head + part, chunk:].astype(F32)

    grad_feat_query, grad_feat_key = run(
        widen_kernel, [(feat_query.shape, F32), (feat_key.shape, F32)], [done]
    )
    return (attended, grad_query, grad_key, grad_value, grad_feat_query, grad_feat_key, grad_gain)


def solution(mesh):
    seq, head = mesh.devices.shape
    split = Mesh(mesh.devices.reshape(seq // NEAR, NEAR, head), ("far", "near", "head"))
    wide = P(("far", "near"), "head")
    per_head = P("head", None, None)
    in_specs = (wide, wide, wide, per_head, per_head, P("head"), wide)
    out_specs = (wide, wide, wide, wide, per_head, per_head, P("head"))
    return jax.shard_map(shards, mesh=split, in_specs=in_specs, out_specs=out_specs, check_vma=False)
```

```python
import jax
import jax.numpy as jnp
from jax import lax
from jax.experimental import pallas as pl
from jax.experimental.pallas import tpu as pltpu
from jax.sharding import Mesh, PartitionSpec as P

EPSILON = 1e-05
BF = jnp.bfloat16
F32 = jnp.float32
NEAR = 8
GAIN_ROWS = 16
STAT_ROWS = 8
TOKEN = ((8, 128), F32)
VMEM_BYTES = 24 * 1024 * 1024
WHOLE_VMEM = 64 * 1024 * 1024


def swap(x, axis):
    return lax.all_to_all(x, axis, 0, 0)


def run(kernel, outs, ins, after=()):
    count = len(ins)

    def body(*refs):
        kernel(*refs[:count], *refs[count + len(after) :])

    whole = pl.BlockSpec(memory_space=pltpu.VMEM)
    return pl.pallas_call(
        body,
        out_shape=[jax.ShapeDtypeStruct(shape, dtype) for shape, dtype in outs],
        in_specs=[whole] * count + [pl.BlockSpec(memory_space=pl.ANY)] * len(after),
        out_specs=[whole] * len(outs),
        compiler_params=pltpu.CompilerParams(vmem_limit_bytes=VMEM_BYTES),
        cost_estimate=pl.CostEstimate(flops=10**8, bytes_accessed=10**6, transcendentals=0),
    )(*ins, *after)


def dot(a, b, over_a, over_b):
    return lax.dot_general(a, b, (((over_a,), (over_b,)), ((), ())), preferred_element_type=F32)


def silu_slope(x):
    g = 1.0 / (1.0 + jnp.exp(-x))
    return g * (1.0 + x * (1.0 - g))


def causal_mask(count, later=0):
    rows = lax.broadcasted_iota(jnp.int32, (count, count), later)
    cols = lax.broadcasted_iota(jnp.int32, (count, count), 1 - later)
    return rows >= cols


def shards(query_rows, key_rows, value_rows, feat_query, feat_key, norm_gain, grad_out):
    tokens, width = query_rows.shape
    heads, size = feat_query.shape[0], feat_query.shape[1]
    near, far = lax.axis_size("near"), lax.axis_size("far")
    full_width = width * lax.axis_size("head")
    chunk = heads * size // near
    slim = chunk // far
    per_head = near // heads
    cols = [slice(h * size, (h + 1) * size) for h in range(heads)]

    def put_state(out_ref, h, value, row):
        for part in range(per_head):
            rows = value[part * chunk : (part + 1) * chunk]
            out_ref[h * per_head + part, row : row + chunk, :] = rows.astype(BF)

    def get_state(ref, h):
        parts = [ref[h * per_head + part] for part in range(per_head)]
        return jnp.concatenate(parts, axis=0)

    quarter = tokens // 4
    blocks = [pl.ds(i * quarter, quarter) for i in range(4)]

    def state_kernel(
        wk_hbm, k_hbm, v_hbm, wq_hbm, q_hbm, gain_hbm, kf_hbm, qf_hbm, out_hbm, row_hbm,
        wk_ref, k_ref, v_ref, wq_ref, q_ref, gain_ref, kf_ref, qf_ref, out_ref, row_ref, in_sems, out_sems,
    ):
        loads, stores = [], []

        def load(source, target):
            move = pltpu.make_async_copy(source, target, in_sems.at[len(loads)])
            move.start()
            loads.append(move)

        def store(source, target):
            move = pltpu.make_async_copy(source, target, out_sems.at[len(stores)])
            move.start()
            stores.append(move)

        def load_rows(source, target):
            for rows in blocks:
                load(source.at[rows, :], target.at[rows, :])

        load(wk_hbm, wk_ref)
        load_rows(k_hbm, k_ref)
        load_rows(v_hbm, v_ref)
        load(wq_hbm, wq_ref)
        load_rows(q_hbm, q_ref)
        load(gain_hbm, gain_ref)
        for move in loads[:5]:
            move.wait()
        for h, at in enumerate(cols):
            pre = dot(k_ref[:, at], wk_ref[h], 1, 0)
            kf_ref[:, at] = (pre / (1.0 + jnp.exp(-pre))).astype(BF)
            store(kf_ref.at[:, at], kf_hbm.at[:, at])
        for move in loads[5:9]:
            move.wait()
        for h, at in enumerate(cols):
            put_state(out_ref, h, dot(kf_ref[:, at], v_ref[:, at], 0, 0), 0)
            own = pl.ds(h * per_head, per_head)
            store(out_ref.at[own], out_hbm.at[own])
        for move in loads[9:]:
            move.wait()
        for h, at in enumerate(cols):
            row_ref[:, at] = jnp.broadcast_to(gain_ref[at].reshape(1, size), (8, size))
        store(row_ref, row_hbm)
        for h, at in enumerate(cols):
            pre = dot(q_ref[:, at], wq_ref[h], 1, 0)
            qf_ref[:, at] = (pre / (1.0 + jnp.exp(-pre))).astype(BF)
            store(qf_ref.at[:, at], qf_hbm.at[:, at])
        for move in stores:
            move.wait()

    anywhere = pl.BlockSpec(memory_space=pl.ANY)
    inputs = [feat_key, key_rows, value_rows, feat_query, query_rows, norm_gain]
    results = [
        jax.ShapeDtypeStruct((tokens, width), BF),
        jax.ShapeDtypeStruct((tokens, width), BF),
        jax.ShapeDtypeStruct((near, chunk, size), BF),
        jax.ShapeDtypeStruct((8, width), F32),
    ]
    key_feat, query_feat, payload, gain_rows = pl.pallas_call(
        state_kernel,
        out_shape=results,
        in_specs=[anywhere] * len(inputs),
        out_specs=[anywhere] * len(results),
        scratch_shapes=[pltpu.VMEM(x.shape, x.dtype) for x in inputs + results]
        + [pltpu.SemaphoreType.DMA((15,)), pltpu.SemaphoreType.DMA((3 * heads + 1,))],
        compiler_params=pltpu.CompilerParams(vmem_limit_bytes=WHOLE_VMEM),
        cost_estimate=pl.CostEstimate(flops=10**8, bytes_accessed=10**6, transcendentals=0),
    )(*inputs)
    parts = swap(payload, "near")

    def total_kernel(in_ref, out_ref):
        total = in_ref[0].astype(F32)
        for i in range(1, near):
            total = total + in_ref[i].astype(F32)
        total = total.astype(BF)
        for i in range(out_ref.shape[0]):
            out_ref[i] = total

    (payload,) = run(total_kernel, [((far, chunk, size), BF)], [parts])
    parts_far = swap(payload, "far")

    def join(parts_ref, far_ref, out_ref, backward):
        place = lax.axis_index("far")
        state = jnp.zeros((chunk, size), F32)
        for i in range(far):
            keep = (i > place) if backward else (i < place)
            state = state + jnp.where(keep, far_ref[i][:chunk].astype(F32), 0.0)
        for i in range(near - 1, -1, -1) if backward else range(near):
            out_ref[i] = state.astype(BF)
            state = state + parts_ref[i][:chunk].astype(F32)

    def prior_kernel(parts_ref, far_ref, out_ref):
        join(parts_ref, far_ref, out_ref, False)

    (payload,) = run(prior_kernel, [((near, chunk, size), BF)], [parts, parts_far])
    prior = swap(payload, "near")

    def norm_kernel(qf_ref, kf_ref, v_ref, p_ref, go_ref, gain_ref, pre_ref, out_ref):
        mask = causal_mask(tokens)
        squares = jnp.zeros((tokens, size), F32)
        inner = jnp.zeros((tokens, size), F32)
        for h, at in enumerate(cols):
            scores = jnp.where(mask, dot(qf_ref[:, at], kf_ref[:, at], 1, 1), 0.0).astype(BF)
            pre = dot(scores, v_ref[:, at], 1, 0) + dot(qf_ref[:, at], get_state(p_ref, h), 1, 0)
            pre_ref[:, at] = pre
            squares = squares + pre * pre
            inner = inner + go_ref[:, at].astype(F32) * gain_ref[:1, at] * pre
        squares = jnp.sum(squares, axis=1, keepdims=True)
        inner = jnp.sum(inner, axis=1, keepdims=True)
        lane = lax.broadcasted_iota(jnp.int32, (tokens, size), 1)
        both = jnp.where(lane == 0, squares, jnp.where(lane == 1, inner, 0.0))
        rows = jnp.transpose(both)[:STAT_ROWS]
        for i in range(out_ref.shape[0]):
            out_ref[i] = rows

    peers = lax.axis_size("head")
    pre_norm, payload = run(
        norm_kernel,
        [((tokens, width), F32), ((peers, STAT_ROWS, tokens), F32)],
        [query_feat, key_feat, value_rows, prior, grad_out, gain_rows],
    )
    stats = swap(payload, "head")

    def slope_kernel(q_ref, wq_ref, k_ref, wk_ref, qs_ref, ks_ref):
        for h, at in enumerate(cols):
            qs_ref[:, at] = silu_slope(dot(q_ref[:, at], wq_ref[h], 1, 0)).astype(BF)
            ks_ref[:, at] = silu_slope(dot(k_ref[:, at], wk_ref[h], 1, 0)).astype(BF)

    query_slope, key_slope = run(
        slope_kernel,
        [((tokens, width), BF), ((tokens, width), BF)],
        [query_rows, feat_query, key_rows, feat_key],
        after=[pre_norm],
    )

    def row_factors(st_ref):
        rows = st_ref[0]
        for i in range(1, peers):
            rows = rows + st_ref[i]
        rows = jnp.concatenate([rows, jnp.zeros((size - STAT_ROWS, tokens), F32)], axis=0)
        both = jnp.transpose(rows)
        inverse = 1.0 / jnp.sqrt(both[:, 0:1] / full_width + EPSILON)
        return inverse, both[:, 1:2] * inverse / full_width

    def query_side(h, at, delta, mask, v_ref, kf_ref, p_ref, qs_ref):
        back = jnp.where(mask, dot(delta, v_ref[:, at], 1, 1), 0.0).astype(BF)
        grad = dot(back, kf_ref[:, at], 1, 0) + dot(delta, get_state(p_ref, h), 1, 1)
        return (grad * qs_ref[:, at].astype(F32)).astype(BF)

    def delta_kernel(
        st_ref, pre_ref, go_ref, gain_ref, qf_ref, v_ref, kf_ref, p_ref, q_ref, qs_ref, att_ref, delta_ref, out_ref
    ):
        inverse, slope = row_factors(st_ref)
        mask = causal_mask(tokens)
        gains = []
        for h, at in enumerate(cols):
            normed = pre_ref[:, at] * inverse
            wide = go_ref[:, at].astype(F32)
            delta = ((wide * gain_ref[:1, at] - normed * slope) * inverse).astype(BF)
            delta_ref[:, at] = delta
            att_ref[:, at] = (normed * gain_ref[:1, at]).astype(BF)
            gains.append(jnp.sum(wide * normed, axis=0, keepdims=True))
            put_state(out_ref, h, dot(qf_ref[:, at], delta, 0, 0), 0)
            grad = query_side(h, at, delta, mask, v_ref, kf_ref, p_ref, qs_ref)
            put_state(out_ref, h, dot(q_ref[:, at], grad, 0, 0), chunk)
        rest = [jnp.zeros((GAIN_ROWS - heads, size), F32)]
        rows = jnp.concatenate(gains + rest, axis=0).astype(BF)
        for i in range(near):
            out_ref[i, 2 * chunk :, :] = rows

    attended_near, delta, payload = run(
        delta_kernel,
        [((tokens, width), BF), ((tokens, width), BF), ((near, 2 * chunk + GAIN_ROWS, size), BF)],
        [stats, pre_norm, grad_out, gain_rows, query_feat, value_rows, key_feat, prior, query_rows, query_slope],
    )
    parts = swap(payload, "near")

    def back_total_kernel(in_ref, out_ref):
        total = in_ref[0].astype(F32)
        for i in range(1, near):
            total = total + in_ref[i].astype(F32)
        head_rows, gains = total[:chunk], total[2 * chunk : 2 * chunk + 8]
        for i in range(far):
            part = total[chunk + i * slim : chunk + (i + 1) * slim]
            out_ref[i] = jnp.concatenate([head_rows, part, gains], axis=0).astype(BF)

    (payload,) = run(
        back_total_kernel, [((far, chunk + slim + 8, size), BF)], [parts]
    )
    parts_far = swap(payload, "far")

    def later_kernel(parts_ref, far_ref, out_ref, side_ref):
        join(parts_ref, far_ref, out_ref, True)
        side = far_ref[0].astype(F32)[chunk:]
        for i in range(1, far):
            side = side + far_ref[i].astype(F32)[chunk:]
        side_ref[...] = side

    payload, side = run(
        later_kernel,
        [((near, chunk, size), BF), ((slim + 8, size), F32)],
        [parts, parts_far],
    )
    later = swap(payload, "near")

    def key_kernel(delta_ref, qf_ref, v_ref, l_ref, ks_ref, k_ref, kpg_ref, out_ref):
        turned = causal_mask(tokens, 1)
        for h, at in enumerate(cols):
            back = jnp.where(turned, dot(v_ref[:, at], delta_ref[:, at], 1, 1), 0.0).astype(BF)
            grad = dot(back, qf_ref[:, at], 1, 0) + dot(v_ref[:, at], get_state(l_ref, h), 1, 1)
            grad = (grad * ks_ref[:, at].astype(F32)).astype(BF)
            kpg_ref[:, at] = grad
            put_state(out_ref, h, dot(k_ref[:, at], grad, 0, 0), 0)

    key_pre_grad, payload = run(
        key_kernel,
        [((tokens, width), BF), ((near, chunk, size), BF)],
        [delta, query_feat, value_rows, later, key_slope, key_rows],
    )
    parts = swap(payload, "near")

    def last_kernel(
        kpg_ref, wk_ref, l_ref, delta_ref, qf_ref, kf_ref, v_ref, p_ref, qs_ref, wq_ref, att_ref, side_ref,
        gk_ref, gq_ref, gv_ref, out_ref, gain_ref, token_ref,
    ):
        out_ref[...] = att_ref[...]
        for h, at in enumerate(cols):
            gain_ref[at] = side_ref[slim + h]
        token_ref[...] = jnp.zeros(token_ref.shape, F32)
        mask, turned = causal_mask(tokens), causal_mask(tokens, 1)
        for h, at in enumerate(cols):
            gk_ref[:, at] = dot(kpg_ref[:, at], wk_ref[h], 1, 1).astype(BF)
            delta = delta_ref[:, at]
            grad = query_side(h, at, delta, mask, v_ref, kf_ref, p_ref, qs_ref)
            gq_ref[:, at] = dot(grad, wq_ref[h], 1, 1).astype(BF)
            scores = jnp.where(turned, dot(kf_ref[:, at], qf_ref[:, at], 1, 1), 0.0).astype(BF)
            value = dot(scores, delta, 1, 0) + dot(kf_ref[:, at], get_state(l_ref, h), 1, 0)
            gv_ref[:, at] = value.astype(BF)

    grad_key, grad_query, grad_value, attended, grad_gain, token = run(
        last_kernel,
        [((tokens, width), BF)] * 4 + [((width,), F32), TOKEN],
        [
            key_pre_grad, feat_key, later, delta, query_feat, key_feat, value_rows, prior, query_slope, feat_query,
            attended_near, side,
        ],
    )

    def weight_total_kernel(in_ref, side_ref, out_ref):
        total = in_ref[0].astype(F32)
        for i in range(1, near):
            total = total + in_ref[i].astype(F32)
        pad = jnp.zeros((8, size), F32)
        total = jnp.concatenate([total, side_ref[:slim], pad], axis=0).astype(BF)
        for i in range(far):
            out_ref[i] = total

    (payload,) = run(
        weight_total_kernel,
        [((far, chunk + slim + 8, size), BF)],
        [parts, side],
        after=[token],
    )
    parts_far = swap(payload, "far")

    def weight_kernel(far_ref, out_ref):
        total = far_ref[0].astype(F32)[:chunk]
        for i in range(1, far):
            total = total + far_ref[i].astype(F32)[:chunk]
        queries = [far_ref[i].astype(F32)[chunk : chunk + slim] for i in range(far)]
        total = jnp.concatenate([total] + queries, axis=0).astype(BF)
        for i in range(near):
            out_ref[i] = total

    (payload,) = run(weight_kernel, [((near, 2 * chunk, size), BF)], [parts_far])
    done = swap(payload, "near")

    def widen_kernel(in_ref, gq_hbm, gk_hbm, gq_ref, gk_ref, sems):
        moves = []
        for h in range(heads):
            for part in range(per_head):
                rows = slice(part * chunk, (part + 1) * chunk)
                gk_ref[h, rows] = in_ref[h * per_head + part, :chunk].astype(F32)
                gq_ref[h, rows] = in_ref[h * per_head + part, chunk:].astype(F32)
            for held, out in ((gk_ref, gk_hbm), (gq_ref, gq_hbm)):
                move = pltpu.make_async_copy(held.at[h], out.at[h], sems.at[len(moves)])
                move.start()
                moves.append(move)
        for move in moves:
            move.wait()

    shapes = [jax.ShapeDtypeStruct(x.shape, F32) for x in (feat_query, feat_key)]
    grad_feat_query, grad_feat_key = pl.pallas_call(
        widen_kernel,
        out_shape=shapes,
        in_specs=[pl.BlockSpec(memory_space=pltpu.VMEM)],
        out_specs=[anywhere] * 2,
        scratch_shapes=[pltpu.VMEM(x.shape, F32) for x in shapes]
        + [pltpu.SemaphoreType.DMA((2 * heads,))],
        compiler_params=pltpu.CompilerParams(vmem_limit_bytes=VMEM_BYTES),
        cost_estimate=pl.CostEstimate(flops=10**6, bytes_accessed=10**6, transcendentals=0),
    )(done)
    return (attended, grad_query, grad_key, grad_value, grad_feat_query, grad_feat_key, grad_gain)


def solution(mesh):
    seq, head = mesh.devices.shape
    split = Mesh(mesh.devices.reshape(seq // NEAR, NEAR, head), ("far", "near", "head"))
    wide = P(("far", "near"), "head")
    per_head = P("head", None, None)
    in_specs = (wide, wide, wide, per_head, per_head, P("head"), wide)
    out_specs = (wide, wide, wide, wide, per_head, per_head, P("head"))
    return jax.shard_map(shards, mesh=split, in_specs=in_specs, out_specs=out_specs, check_vma=False)
```

```python
import jax
import jax.numpy as jnp
from jax import lax
from jax.experimental import pallas as pl
from jax.experimental.pallas import tpu as pltpu
from jax.sharding import Mesh, PartitionSpec as P

EPSILON = 1e-05
BF = jnp.bfloat16
F32 = jnp.float32
NEAR = 8
GAIN_ROWS = 16
STAT_ROWS = 8
TOKEN = ((8, 128), F32)
VMEM_BYTES = 24 * 1024 * 1024
WHOLE_VMEM = 64 * 1024 * 1024


def swap(x, axis):
    return lax.all_to_all(x, axis, 0, 0)


def run(kernel, outs, ins, after=()):
    count = len(ins)

    def body(*refs):
        kernel(*refs[:count], *refs[count + len(after) :])

    whole = pl.BlockSpec(memory_space=pltpu.VMEM)
    return pl.pallas_call(
        body,
        out_shape=[jax.ShapeDtypeStruct(shape, dtype) for shape, dtype in outs],
        in_specs=[whole] * count + [pl.BlockSpec(memory_space=pl.ANY)] * len(after),
        out_specs=[whole] * len(outs),
        compiler_params=pltpu.CompilerParams(vmem_limit_bytes=VMEM_BYTES),
        cost_estimate=pl.CostEstimate(flops=10**8, bytes_accessed=10**6, transcendentals=0),
    )(*ins, *after)


def dot(a, b, over_a, over_b):
    return lax.dot_general(a, b, (((over_a,), (over_b,)), ((), ())), preferred_element_type=F32)


def silu(x):
    half = 0.5 * x
    return half + half * jnp.tanh(half)


def silu_slope(x):
    g = 0.5 + 0.5 * jnp.tanh(0.5 * x)
    return g * (1.0 + x * (1.0 - g))


def causal_mask(count, later=0):
    rows = lax.broadcasted_iota(jnp.int32, (count, count), later)
    cols = lax.broadcasted_iota(jnp.int32, (count, count), 1 - later)
    return rows >= cols


def shards(query_rows, key_rows, value_rows, feat_query, feat_key, norm_gain, grad_out):
    tokens, width = query_rows.shape
    heads, size = feat_query.shape[0], feat_query.shape[1]
    near, far = lax.axis_size("near"), lax.axis_size("far")
    full_width = width * lax.axis_size("head")
    chunk = heads * size // near
    slim = chunk // far
    per_head = near // heads
    cols = [slice(h * size, (h + 1) * size) for h in range(heads)]

    def put_state(out_ref, h, value, row):
        for part in range(per_head):
            rows = value[part * chunk : (part + 1) * chunk]
            out_ref[h * per_head + part, row : row + chunk, :] = rows.astype(BF)

    def get_state(ref, h):
        parts = [ref[h * per_head + part] for part in range(per_head)]
        return jnp.concatenate(parts, axis=0)

    quarter = tokens // 4
    blocks = [pl.ds(i * quarter, quarter) for i in range(4)]

    def state_kernel(
        wk_hbm, k_hbm, v_hbm, wq_hbm, q_hbm, gain_hbm, kf_hbm, qf_hbm, out_hbm, row_hbm,
        wk_ref, k_ref, v_ref, wq_ref, q_ref, gain_ref, kf_ref, qf_ref, out_ref, row_ref, in_sems, out_sems,
    ):
        loads, stores = [], []

        def load(source, target):
            move = pltpu.make_async_copy(source, target, in_sems.at[len(loads)])
            move.start()
            loads.append(move)

        def store(source, target):
            move = pltpu.make_async_copy(source, target, out_sems.at[len(stores)])
            move.start()
            stores.append(move)

        def load_rows(source, target):
            for rows in blocks:
                load(source.at[rows, :], target.at[rows, :])

        load(wk_hbm, wk_ref)
        load_rows(k_hbm, k_ref)
        load_rows(v_hbm, v_ref)
        load(wq_hbm, wq_ref)
        load_rows(q_hbm, q_ref)
        load(gain_hbm, gain_ref)
        for move in loads[:5]:
            move.wait()
        for h, at in enumerate(cols):
            pre = dot(k_ref[:, at], wk_ref[h], 1, 0)
            kf_ref[:, at] = silu(pre).astype(BF)
            store(kf_ref.at[:, at], kf_hbm.at[:, at])
        for move in loads[5:9]:
            move.wait()
        for h, at in enumerate(cols):
            put_state(out_ref, h, dot(kf_ref[:, at], v_ref[:, at], 0, 0), 0)
            own = pl.ds(h * per_head, per_head)
            store(out_ref.at[own], out_hbm.at[own])
        for move in loads[9:]:
            move.wait()
        for h, at in enumerate(cols):
            row_ref[:, at] = jnp.broadcast_to(gain_ref[at].reshape(1, size), (8, size))
        store(row_ref, row_hbm)
        for h, at in enumerate(cols):
            pre = dot(q_ref[:, at], wq_ref[h], 1, 0)
            qf_ref[:, at] = silu(pre).astype(BF)
            store(qf_ref.at[:, at], qf_hbm.at[:, at])
        for move in stores:
            move.wait()

    anywhere = pl.BlockSpec(memory_space=pl.ANY)
    inputs = [feat_key, key_rows, value_rows, feat_query, query_rows, norm_gain]
    results = [
        jax.ShapeDtypeStruct((tokens, width), BF),
        jax.ShapeDtypeStruct((tokens, width), BF),
        jax.ShapeDtypeStruct((near, chunk, size), BF),
        jax.ShapeDtypeStruct((8, width), F32),
    ]
    key_feat, query_feat, payload, gain_rows = pl.pallas_call(
        state_kernel,
        out_shape=results,
        in_specs=[anywhere] * len(inputs),
        out_specs=[anywhere] * len(results),
        scratch_shapes=[pltpu.VMEM(x.shape, x.dtype) for x in inputs + results]
        + [pltpu.SemaphoreType.DMA((15,)), pltpu.SemaphoreType.DMA((3 * heads + 1,))],
        compiler_params=pltpu.CompilerParams(vmem_limit_bytes=WHOLE_VMEM),
        cost_estimate=pl.CostEstimate(flops=10**8, bytes_accessed=10**6, transcendentals=0),
    )(*inputs)
    parts = swap(payload, "near")

    def total_kernel(in_ref, out_ref):
        total = in_ref[0].astype(F32)
        for i in range(1, near):
            total = total + in_ref[i].astype(F32)
        total = total.astype(BF)
        for i in range(out_ref.shape[0]):
            out_ref[i] = total

    (payload,) = run(total_kernel, [((far, chunk, size), BF)], [parts])
    parts_far = swap(payload, "far")

    def join(parts_ref, far_ref, out_ref, backward):
        place = lax.axis_index("far")
        state = jnp.zeros((chunk, size), F32)
        for i in range(far):
            keep = (i > place) if backward else (i < place)
            state = state + jnp.where(keep, far_ref[i][:chunk].astype(F32), 0.0)
        for i in range(near - 1, -1, -1) if backward else range(near):
            out_ref[i] = state.astype(BF)
            state = state + parts_ref[i][:chunk].astype(F32)

    def prior_kernel(parts_ref, far_ref, out_ref):
        join(parts_ref, far_ref, out_ref, False)

    (payload,) = run(prior_kernel, [((near, chunk, size), BF)], [parts, parts_far])
    prior = swap(payload, "near")

    def norm_kernel(qf_ref, kf_ref, v_ref, p_ref, go_ref, gain_ref, pre_ref, out_ref):
        mask = causal_mask(tokens)
        squares = jnp.zeros((tokens, size), F32)
        inner = jnp.zeros((tokens, size), F32)
        for h, at in enumerate(cols):
            scores = jnp.where(mask, dot(qf_ref[:, at], kf_ref[:, at], 1, 1), 0.0).astype(BF)
            pre = dot(scores, v_ref[:, at], 1, 0) + dot(qf_ref[:, at], get_state(p_ref, h), 1, 0)
            pre_ref[:, at] = pre
            squares = squares + pre * pre
            inner = inner + go_ref[:, at].astype(F32) * gain_ref[:1, at] * pre
        squares = jnp.sum(squares, axis=1, keepdims=True)
        inner = jnp.sum(inner, axis=1, keepdims=True)
        lane = lax.broadcasted_iota(jnp.int32, (tokens, size), 1)
        both = jnp.where(lane == 0, squares, jnp.where(lane == 1, inner, 0.0))
        rows = jnp.transpose(both)[:STAT_ROWS]
        for i in range(out_ref.shape[0]):
            out_ref[i] = rows

    peers = lax.axis_size("head")
    pre_norm, payload = run(
        norm_kernel,
        [((tokens, width), F32), ((peers, STAT_ROWS, tokens), F32)],
        [query_feat, key_feat, value_rows, prior, grad_out, gain_rows],
    )
    stats = swap(payload, "head")

    def row_factors(st_ref):
        rows = st_ref[0]
        for i in range(1, peers):
            rows = rows + st_ref[i]
        rows = jnp.concatenate([rows, jnp.zeros((size - STAT_ROWS, tokens), F32)], axis=0)
        both = jnp.transpose(rows)
        inverse = 1.0 / jnp.sqrt(both[:, 0:1] / full_width + EPSILON)
        return inverse, both[:, 1:2] * inverse / full_width

    def query_side(h, at, delta, mask, v_ref, kf_ref, p_ref, q_ref, wq_ref):
        back = jnp.where(mask, dot(delta, v_ref[:, at], 1, 1), 0.0).astype(BF)
        grad = dot(back, kf_ref[:, at], 1, 0) + dot(delta, get_state(p_ref, h), 1, 1)
        return (grad * silu_slope(dot(q_ref[:, at], wq_ref[h], 1, 0))).astype(BF)

    def delta_kernel(
        st_ref, pre_ref, go_ref, gain_ref, qf_ref, v_ref, kf_ref, p_ref, q_ref, wq_ref, att_ref, delta_ref, out_ref
    ):
        inverse, slope = row_factors(st_ref)
        mask = causal_mask(tokens)
        gains = []
        for h, at in enumerate(cols):
            normed = pre_ref[:, at] * inverse
            wide = go_ref[:, at].astype(F32)
            delta = ((wide * gain_ref[:1, at] - normed * slope) * inverse).astype(BF)
            delta_ref[:, at] = delta
            att_ref[:, at] = (normed * gain_ref[:1, at]).astype(BF)
            gains.append(jnp.sum(wide * normed, axis=0, keepdims=True))
            put_state(out_ref, h, dot(qf_ref[:, at], delta, 0, 0), 0)
            grad = query_side(h, at, delta, mask, v_ref, kf_ref, p_ref, q_ref, wq_ref)
            put_state(out_ref, h, dot(q_ref[:, at], grad, 0, 0), chunk)
        rest = [jnp.zeros((GAIN_ROWS - heads, size), F32)]
        rows = jnp.concatenate(gains + rest, axis=0).astype(BF)
        for i in range(near):
            out_ref[i, 2 * chunk :, :] = rows

    attended_near, delta, payload = run(
        delta_kernel,
        [((tokens, width), BF), ((tokens, width), BF), ((near, 2 * chunk + GAIN_ROWS, size), BF)],
        [stats, pre_norm, grad_out, gain_rows, query_feat, value_rows, key_feat, prior, query_rows, feat_query],
    )
    parts = swap(payload, "near")

    def back_total_kernel(in_ref, out_ref):
        total = in_ref[0].astype(F32)
        for i in range(1, near):
            total = total + in_ref[i].astype(F32)
        head_rows, gains = total[:chunk], total[2 * chunk : 2 * chunk + 8]
        for i in range(far):
            part = total[chunk + i * slim : chunk + (i + 1) * slim]
            out_ref[i] = jnp.concatenate([head_rows, part, gains], axis=0).astype(BF)

    (payload,) = run(
        back_total_kernel, [((far, chunk + slim + 8, size), BF)], [parts]
    )
    parts_far = swap(payload, "far")

    def later_kernel(parts_ref, far_ref, out_ref, side_ref):
        join(parts_ref, far_ref, out_ref, True)
        side = far_ref[0].astype(F32)[chunk:]
        for i in range(1, far):
            side = side + far_ref[i].astype(F32)[chunk:]
        side_ref[...] = side

    payload, side = run(
        later_kernel,
        [((near, chunk, size), BF), ((slim + 8, size), F32)],
        [parts, parts_far],
    )
    later = swap(payload, "near")

    def key_kernel(delta_ref, qf_ref, v_ref, l_ref, wk_ref, k_ref, kpg_ref, out_ref):
        turned = causal_mask(tokens, 1)
        for h, at in enumerate(cols):
            back = jnp.where(turned, dot(v_ref[:, at], delta_ref[:, at], 1, 1), 0.0).astype(BF)
            grad = dot(back, qf_ref[:, at], 1, 0) + dot(v_ref[:, at], get_state(l_ref, h), 1, 1)
            grad = (grad * silu_slope(dot(k_ref[:, at], wk_ref[h], 1, 0))).astype(BF)
            kpg_ref[:, at] = grad
            put_state(out_ref, h, dot(k_ref[:, at], grad, 0, 0), 0)

    key_pre_grad, payload = run(
        key_kernel,
        [((tokens, width), BF), ((near, chunk, size), BF)],
        [delta, query_feat, value_rows, later, feat_key, key_rows],
    )
    parts = swap(payload, "near")

    def last_kernel(
        kpg_ref, wk_ref, l_ref, delta_ref, qf_ref, kf_ref, v_ref, p_ref, q_ref, wq_ref, att_ref, side_ref,
        gk_ref, gq_ref, gv_ref, out_ref, gain_ref, token_ref,
    ):
        out_ref[...] = att_ref[...]
        for h, at in enumerate(cols):
            gain_ref[at] = side_ref[slim + h]
        token_ref[...] = jnp.zeros(token_ref.shape, F32)
        mask, turned = causal_mask(tokens), causal_mask(tokens, 1)
        for h, at in enumerate(cols):
            gk_ref[:, at] = dot(kpg_ref[:, at], wk_ref[h], 1, 1).astype(BF)
            delta = delta_ref[:, at]
            grad = query_side(h, at, delta, mask, v_ref, kf_ref, p_ref, q_ref, wq_ref)
            gq_ref[:, at] = dot(grad, wq_ref[h], 1, 1).astype(BF)
            scores = jnp.where(turned, dot(kf_ref[:, at], qf_ref[:, at], 1, 1), 0.0).astype(BF)
            value = dot(scores, delta, 1, 0) + dot(kf_ref[:, at], get_state(l_ref, h), 1, 0)
            gv_ref[:, at] = value.astype(BF)

    grad_key, grad_query, grad_value, attended, grad_gain, token = run(
        last_kernel,
        [((tokens, width), BF)] * 4 + [((width,), F32), TOKEN],
        [
            key_pre_grad, feat_key, later, delta, query_feat, key_feat, value_rows, prior, query_rows, feat_query,
            attended_near, side,
        ],
    )

    def weight_total_kernel(in_ref, side_ref, out_ref):
        total = in_ref[0].astype(F32)
        for i in range(1, near):
            total = total + in_ref[i].astype(F32)
        pad = jnp.zeros((8, size), F32)
        total = jnp.concatenate([total, side_ref[:slim], pad], axis=0).astype(BF)
        for i in range(far):
            out_ref[i] = total

    (payload,) = run(
        weight_total_kernel,
        [((far, chunk + slim + 8, size), BF)],
        [parts, side],
        after=[token],
    )
    parts_far = swap(payload, "far")

    def weight_kernel(far_ref, out_ref):
        total = far_ref[0].astype(F32)[:chunk]
        for i in range(1, far):
            total = total + far_ref[i].astype(F32)[:chunk]
        queries = [far_ref[i].astype(F32)[chunk : chunk + slim] for i in range(far)]
        total = jnp.concatenate([total] + queries, axis=0).astype(BF)
        for i in range(near):
            out_ref[i] = total

    (payload,) = run(weight_kernel, [((near, 2 * chunk, size), BF)], [parts_far])
    done = swap(payload, "near")

    def widen_kernel(in_ref, gq_ref, gk_ref):
        for h in range(heads):
            for part in range(per_head):
                rows = slice(part * chunk, (part + 1) * chunk)
                gk_ref[h, rows] = in_ref[h * per_head + part, :chunk].astype(F32)
                gq_ref[h, rows] = in_ref[h * per_head + part, chunk:].astype(F32)

    grad_feat_query, grad_feat_key = run(
        widen_kernel, [(feat_query.shape, F32), (feat_key.shape, F32)], [done]
    )
    return (attended, grad_query, grad_key, grad_value, grad_feat_query, grad_feat_key, grad_gain)


def solution(mesh):
    seq, head = mesh.devices.shape
    split = Mesh(mesh.devices.reshape(seq // NEAR, NEAR, head), ("far", "near", "head"))
    wide = P(("far", "near"), "head")
    per_head = P("head", None, None)
    in_specs = (wide, wide, wide, per_head, per_head, P("head"), wide)
    out_specs = (wide, wide, wide, wide, per_head, per_head, P("head"))
    return jax.shard_map(shards, mesh=split, in_specs=in_specs, out_specs=out_specs, check_vma=False)
```
